128 devices in a mesh: section: 2 (over core), ep: 64 (over y, x, z).
Axes of the slice: x: 4, y: 4, z: 4, core: 2. Of those that a mesh axis runs over, the one named last changes fastest.
Arguments:
- top_grads: bfloat16 [2, 4096, 1536], P(None, 'ep'), may hold values from -6 to 6
- expert_ids: int32 [2, 2, 4096, 4], P('section', None, 'ep'), may hold values from 0 to 63, as said below
- route_weights: float32 [2, 2, 4096, 4], P('section', None, 'ep'), may hold values from 0.05 to 0.6
- preacts: bfloat16 [2, 2, 64, 384, 3072], P('section', None, 'ep'), may hold values from -6 to 6
- w_gate_up: bfloat16 [2, 64, 1536, 3072], P('section', 'ep'), may hold values from -0.15625 to 0.15625
- w_down: bfloat16 [2, 64, 1536, 1536], P('section', 'ep'), may hold values from -0.15625 to 0.15625
Outputs:
- input_grads: bfloat16 [2, 2, 4096, 1536], P('section', None, 'ep')
The draws below stay inside these ranges and needn't reach their ends.
Inputs may be any that keep to these rules, and one draw needn't show every extreme that they name: `expert_ids`: each row names 4 different experts. Among the rows of one block of 64 tokens of one layer and micro-batch no expert is named more than 6 times, and in each layer and micro-batch some expert is named exactly 6 times in every block.
All inputs are finite; a program needn't handle non-finite values.
Results may differ from the reference program's by a relative error of at most 0.007.
Values may be sent and summed in bfloat16 or wider, within the bound.
No kernel may reach another device: no remote copies, remote signals or barrier semaphores. Data moves between devices by JAX's collectives and lax.ppermute only.
A program may use at most 128 MiB of HBM per device.

```python
import jax
import jax.numpy as jnp
from jax import lax

D = 1536
FF = 1536
TOP = 4
MB = 2
TOK_DEV = 64
LAYERS = 2
EXPERTS = 64
TOKENS = 4096
CAP = 6
SLOTS = 384
N_EP = 64


def draw_expert_ids(key, part):
    key = jax.random.fold_in(key, 11)

    def one_block(block_key, relabel):
        key_pick, key_rows, key_cols = jax.random.split(block_key, 3)
        pool_ids = jnp.repeat(jnp.arange(N_EP - 1, dtype=jnp.int32), CAP)
        chosen = jax.random.permutation(key_pick, pool_ids)[:TOK_DEV * TOP - CAP]
        labels = jnp.concatenate([jnp.sort(chosen), jnp.full((CAP,), N_EP - 1, jnp.int32)])
        grid_ids = labels.reshape(TOP, TOK_DEV).T
        grid_ids = grid_ids[jax.random.permutation(key_rows, TOK_DEV)]
        scores = jax.random.randint(key_cols, (TOK_DEV, TOP), 0, 1024, dtype=jnp.int32) * TOP + jnp.arange(TOP, dtype=jnp.int32)
        column_order = jnp.argsort(scores, axis=1)
        grid_ids = jnp.take_along_axis(grid_ids, column_order, axis=1)
        return relabel[grid_ids].astype(jnp.int32)

    def one_group(group_key):
        relabel = jax.random.permutation(jax.random.fold_in(group_key, 7), N_EP).astype(jnp.int32)
        block_keys = jax.random.split(jax.random.fold_in(group_key, 5), N_EP)
        return jax.vmap(lambda block_key: one_block(block_key, relabel))(block_keys)
    group_keys = jax.random.split(key, LAYERS * MB)
    drawn = jax.vmap(one_group)(group_keys)
    return drawn.reshape(LAYERS, MB, N_EP * TOK_DEV, TOP).astype(jnp.int32)


def level_of(rng, extent, cuts, smallest, top_value):
    def one(dim, blocks):
        steps = jax.random.uniform(jax.random.fold_in(jax.random.fold_in(rng, 6), dim), (blocks,), jnp.float32, smallest / len(cuts), top_value / len(cuts))
        return jnp.repeat(jnp.exp(steps), extent[dim] // blocks).reshape((-1,) + (1,) * (len(extent) - dim - 1))

    factor_of = one(*cuts[0])
    for cut in cuts[1:]:
        factor_of = factor_of * one(*cut)
    return factor_of


def centred(key, shape, width, bound, cuts=(), kind=jnp.bfloat16):
    factor_of = level_of(key, shape, cuts, -0.22, 0.18) if cuts else 1.0
    values = jax.random.normal(key, shape, jnp.float32) * width * factor_of
    return jnp.minimum(jnp.maximum(values, -bound), bound).astype(kind)


def setup_inputs(seed: int = 0) -> dict:
    keys = jax.random.split(jax.random.key(seed), 7)
    return {
        "top_grads": centred(keys[0], (MB, TOKENS, D), 1.0, 6.0, ((1, 64),)),
        "expert_ids": draw_expert_ids(jax.random.fold_in(keys[6], 71), 0),
        "route_weights": jnp.clip(0.05 + 0.55 * jax.random.uniform(keys[2], (LAYERS, MB, TOKENS, TOP), jnp.float32) ** level_of(keys[2], (LAYERS, MB, TOKENS, TOP), ((0, 2), (2, 64)), -0.2, 0.2), 0.05, 0.6),
        "preacts": centred(keys[3], (LAYERS, MB, EXPERTS, SLOTS, 2 * FF), 1.0, 6.0, ((0, 2), (2, 64))),
        "w_gate_up": centred(keys[4], (LAYERS, EXPERTS, D, 2 * FF), D ** -0.5, 0.15625, ((0, 2), (1, 64))),
        "w_down": centred(keys[5], (LAYERS, EXPERTS, FF, D), FF ** -0.5, 0.15625, ((0, 2), (1, 64))),
    }


alpha_glu = 1.702


def destinations(chosen_ids, device_count, capacity):
    flat_ids = chosen_ids.reshape(chosen_ids.shape[:-2] + (chosen_ids.shape[-2] * chosen_ids.shape[-1],))
    one_hot = (flat_ids[..., None] == jnp.arange(device_count, dtype=jnp.int32)).astype(jnp.int32)
    earlier = jnp.cumsum(one_hot, axis=-2, dtype=jnp.int32) - one_hot
    slot_index = jnp.sum(earlier * one_hot, axis=-1, dtype=jnp.int32)
    return (flat_ids * capacity + slot_index).astype(jnp.int32)


def expert_rows(saved, grad_rows, w_gate_up, w_down):
    hidden = w_down.shape[0]
    back_grad = lax.dot_general(grad_rows, w_down, (((1,), (1,)), ((), ())), preferred_element_type=jnp.float32)
    gate_pre = saved[:, :hidden].astype(jnp.float32)
    up_pre = saved[:, hidden:].astype(jnp.float32)
    sigmoid_gate = jax.nn.sigmoid(alpha_glu * gate_pre)
    up_grad = (back_grad * gate_pre * sigmoid_gate).astype(jnp.bfloat16)
    gate_grad = (back_grad * (up_pre + 1.0) * sigmoid_gate * (1.0 + alpha_glu * gate_pre * (1.0 - sigmoid_gate))).astype(jnp.bfloat16)
    joined = jnp.concatenate([gate_grad, up_grad], axis=1)
    return lax.dot_general(joined, w_gate_up, (((1,), (1,)), ((), ())), preferred_element_type=jnp.float32).astype(jnp.bfloat16)


def layer(incoming, chosen_ids, pick_weights, saved, w_gate_up, w_down):
    blocks = chosen_ids.reshape(N_EP, TOK_DEV, TOP)
    targets = lax.map(lambda block_ids: destinations(block_ids, EXPERTS, CAP), blocks)
    experts_of = blocks.reshape(N_EP, TOK_DEV * TOP)
    sources = jnp.arange(N_EP, dtype=jnp.int32)[:, None]
    rows_of = (sources * CAP + (targets - experts_of * CAP)).astype(jnp.int32)
    tokens_of = (sources * TOK_DEV + jnp.arange(TOK_DEV * TOP, dtype=jnp.int32)[None, :] // TOP).astype(jnp.int32)
    scaled = (pick_weights.reshape(N_EP, TOK_DEV * TOP)[..., None] * incoming[tokens_of].astype(jnp.float32)).astype(jnp.bfloat16)
    buffers = jnp.zeros((EXPERTS, SLOTS, D), jnp.bfloat16).at[experts_of, rows_of].set(scaled)
    answers = lax.map(lambda item: expert_rows(item[0], item[1], item[2], item[3]), (saved, buffers, w_gate_up, w_down))
    picked = answers[experts_of, rows_of]
    summed = incoming.astype(jnp.float32) + jnp.sum(picked.astype(jnp.float32).reshape(TOKENS, TOP, D), axis=1)
    return summed.astype(jnp.bfloat16)


def reference(top_grads, expert_ids, route_weights, preacts, w_gate_up, w_down):
    results = [None] * LAYERS
    incoming = top_grads
    for layer_index in range(LAYERS - 1, -1, -1):
        outputs = []
        for micro_index in range(MB):
            outputs.append(layer(incoming[micro_index], expert_ids[layer_index, micro_index], route_weights[layer_index, micro_index], preacts[layer_index, micro_index], w_gate_up[layer_index], w_down[layer_index]))
        incoming = jnp.stack(outputs)
        results[layer_index] = incoming
    return jnp.stack(results)
```

```python
import jax
import jax.numpy as jnp
from jax import lax
from jax.experimental import pallas as pl
from jax.experimental.pallas import tpu as pltpu
from jax.sharding import PartitionSpec as P

alpha_glu = 1.702
BF = jnp.bfloat16
F32 = jnp.float32

MODEL = 1536
HIDDEN = 1536
TOKENS = 64
EXPERTS = 64
TOP = 4
CAP = 6
SLOTS = EXPERTS * CAP
PACK = 8
PART = MODEL // 4
WIDE = 3 * PART
ROWS = EXPERTS * PACK
BLOCKS = 16
GROUP_SLOTS = BLOCKS * CAP
GROUP_ROWS = BLOCKS * PACK
GROUPS = EXPERTS // BLOCKS
TILE = 256
STEPS = HIDDEN // TILE
BIG = 48 * 1024 * 1024


def iota(shape, axis):
    return lax.broadcasted_iota(jnp.int32, shape, axis)


def dot(a, b, contract=((1,), (0,))):
    return lax.dot_general(a, b, (contract, ((), ())), preferred_element_type=F32)


def chosen_meta(layer, own_ref, got_ref):
    section = lax.axis_index("section")
    own = own_ref[:, pl.ds(section, 1)]
    got = got_ref[:, pl.ds(section, 1)]
    both = jnp.where(section == layer, own, got)
    return both[0, 0], both[1, 0]


def named(ids, shape):
    expert = (iota(shape, 0) // PACK).astype(F32)
    return [ids[k : k + 1, :] == expert for k in range(TOP)]


def slot_counts(picked, lanes):
    earlier = (iota((TOKENS, lanes), 0) < (iota((TOKENS, lanes), 1) % TOKENS)).astype(BF)
    return dot(picked.astype(BF), earlier)


def wanted_slots(shape, part):
    row = iota(shape, 0) % PACK
    main = row
    extra = jnp.where(row >= CAP, 3 * (row - CAP) + part, -1)
    return main, extra


def send_masks(ids, weights):
    shape = (ROWS, 4 * TOKENS)
    hits = named(ids, shape)
    weight = jnp.zeros(shape, F32)
    for k in range(TOP):
        weight = weight + jnp.where(hits[k], weights[k : k + 1, :], 0.0)
    picked = hits[0] | hits[1] | hits[2] | hits[3]
    counts = slot_counts(jnp.where(picked, 1.0, 0.0)[:, :TOKENS], 4 * TOKENS)
    counts = jnp.where(picked, counts, -2.0)
    lead = weight.astype(BF).astype(F32)
    group = iota(shape, 1) // TOKENS
    value = jnp.where(group < 2, lead, weight - lead)
    masks = []
    for part in range(3):
        main, extra = wanted_slots(shape, part)
        slot = jnp.where(group % 2 == 0, main, extra).astype(F32)
        masks.append(jnp.where(counts == slot, value, 0.0).astype(BF))
    return masks


def gather_masks(ids):
    shape = (ROWS, 2 * TOKENS)
    hits = named(ids, shape)
    picked = hits[0] | hits[1] | hits[2] | hits[3]
    counts = slot_counts(jnp.where(picked, 1.0, 0.0)[:, :TOKENS], 2 * TOKENS)
    counts = jnp.where(picked, counts, -2.0)
    group = iota(shape, 1) // TOKENS
    masks = []
    for part in range(3):
        main, extra = wanted_slots(shape, part)
        slot = jnp.where(group == 0, main, extra).astype(F32)
        masks.append(jnp.where(counts == slot, 1.0, 0.0))
    return masks


def send_rows(masks, grads, out_ref):
    last = grads[:, WIDE:]
    for part in range(3):
        here = grads[:, part * PART : (part + 1) * PART]
        rows = jnp.concatenate([here, last, here, last], axis=0)
        out_ref[:, part * PART : (part + 1) * PART] = dot(masks[part], rows).astype(BF)


def gather_rows(masks_ref, packed_ref, grads):
    pieces = []
    last = jnp.zeros((TOKENS, PART), F32)
    for part in range(3):
        both = dot(masks_ref[part], packed_ref[:, part * PART : (part + 1) * PART])
        pieces.append(both[:TOKENS])
        last = last + both[TOKENS:]
    total = jnp.concatenate(pieces + [last], axis=1)
    return (grads.astype(F32) + total).astype(BF)


def first_kernel(own_ref, got_ref, grads_ref, out_ref):
    ids, weights = chosen_meta(1, own_ref, got_ref)
    section = lax.axis_index("section")
    send_rows(send_masks(ids, weights), grads_ref[section], out_ref)


def routes_kernel(own_ref, got_ref, send_ref, gather_one_ref, gather_zero_ref):
    ids, _ = chosen_meta(1, own_ref, got_ref)
    for part, mask in enumerate(gather_masks(ids[:, : 2 * TOKENS])):
        gather_one_ref[part] = mask.T.astype(BF)
    ids, weights = chosen_meta(0, own_ref, got_ref)
    for part, mask in enumerate(gather_masks(ids[:, : 2 * TOKENS])):
        gather_zero_ref[part] = mask.T.astype(BF)
    for part, mask in enumerate(send_masks(ids, weights)):
        send_ref[part] = mask


def relay_kernel(packed_ref, gather_ref, send_ref, grads_ref, lower_ref, out_ref):
    section = lax.axis_index("section")
    lower = gather_rows(gather_ref, packed_ref, grads_ref[section])
    lower_ref[...] = lower
    send_rows([send_ref[part] for part in range(3)], lower, out_ref)


def last_kernel(packed_ref, gather_ref, grads_ref, out_ref):
    out_ref[...] = gather_rows(gather_ref, packed_ref, grads_ref[...])


def group_masks():
    shape = (GROUP_ROWS, GROUP_SLOTS)
    row, column = iota(shape, 0), iota(shape, 1)
    block = (column * 43) >> 8
    slot = column - CAP * block
    same = (row >> 3) == block
    inner = row & 7
    main = same & (inner == slot)
    extra = [same & (inner >= CAP) & (slot == 3 * (inner - CAP) + part) for part in range(3)]
    return [jnp.where(mask, 1.0, 0.0) for mask in [main] + extra]


def expert_kernel(
    layer, packed_ref, own_pre, got_pre, own_down, got_down, own_up, got_up,
    out_ref, pre, down, up, rows, joined, answers, sems,
):
    section = lax.axis_index("section")

    def copies(from_pre, from_down, from_up):
        made = []
        for step in range(STEPS):
            here = pl.ds(step * TILE, TILE)
            there = pl.ds(HIDDEN + step * TILE, TILE)
            made.append(pltpu.make_async_copy(from_down.at[here], down.at[here], sems.at[0, step]))
            made.append(pltpu.make_async_copy(from_pre.at[:, here], pre.at[:, here], sems.at[1, step]))
            made.append(pltpu.make_async_copy(from_pre.at[:, there], pre.at[:, there], sems.at[2, step]))
        for step in range(STEPS):
            here = pl.ds(step * TILE, TILE)
            made.append(pltpu.make_async_copy(from_up.at[here], up.at[here], sems.at[3, step]))
        return made

    @pl.when(section == layer)
    def _():
        for copy in copies(own_pre.at[layer], own_down, own_up):
            copy.start()

    @pl.when(section != layer)
    def _():
        for copy in copies(got_pre, got_down, got_up):
            copy.start()

    waits = copies(got_pre, got_down, got_up)
    masks = group_masks()
    pack_masks = [
        jnp.concatenate([masks[0], masks[1 + part]], axis=1).astype(BF) for part in range(3)
    ]
    open_main = masks[0].T.astype(BF)
    open_last = jnp.concatenate([masks[1 + part].T for part in range(3)], axis=1).astype(BF)
    for group in range(GROUPS):
        taken = packed_ref[group * GROUP_ROWS : (group + 1) * GROUP_ROWS, :]
        target = slice(group * GROUP_SLOTS, (group + 1) * GROUP_SLOTS)
        rows[target, :WIDE] = dot(open_main, taken).astype(BF)
        stacked = jnp.concatenate(
            [taken[:, part * PART : (part + 1) * PART] for part in range(3)], axis=0
        )
        rows[target, WIDE:] = dot(open_last, stacked).astype(BF)

    for step in range(STEPS):
        here = slice(step * TILE, (step + 1) * TILE)
        there = slice(HIDDEN + step * TILE, HIDDEN + (step + 1) * TILE)
        for copy in waits[3 * step : 3 * step + 3]:
            copy.wait()
        back = dot(rows[...], down[here, :], ((1,), (1,)))
        gate = pre[:, here].astype(F32)
        linear = pre[:, there].astype(F32)
        sigmoid = jax.nn.sigmoid(alpha_glu * gate)
        joined[:, there] = (back * gate * sigmoid).astype(BF)
        joined[:, here] = (
            back * (linear + 1.0) * sigmoid * (1.0 + alpha_glu * gate * (1.0 - sigmoid))
        ).astype(BF)
    for step in range(STEPS):
        here = slice(step * TILE, (step + 1) * TILE)
        waits[3 * STEPS + step].wait()
        answers[:, here] = dot(joined[...], up[here, :], ((1,), (1,))).astype(BF)
    for group in range(GROUPS):
        source = slice(group * GROUP_SLOTS, (group + 1) * GROUP_SLOTS)
        target = slice(group * GROUP_ROWS, (group + 1) * GROUP_ROWS)
        last = answers[source, WIDE:]
        for part in range(3):
            columns = slice(part * PART, (part + 1) * PART)
            both = jnp.concatenate([answers[source, columns], last], axis=0)
            out_ref[target, columns] = dot(pack_masks[part], both).astype(BF)


def shape(*dims, dtype=BF):
    return jax.ShapeDtypeStruct(dims, dtype)


def small_call(kernel, outs, name, flops):
    return pl.pallas_call(
        kernel,
        out_shape=outs,
        name=name,
        compiler_params=pltpu.CompilerParams(vmem_limit_bytes=24 * 1024 * 1024),
        cost_estimate=pl.CostEstimate(flops=flops, bytes_accessed=4_000_000, transcendentals=0),
    )


def expert_call(layer):
    whole = pl.BlockSpec(memory_space=pltpu.VMEM)
    far = pl.BlockSpec(memory_space=pl.ANY)
    return pl.pallas_call(
        lambda *refs: expert_kernel(layer, *refs),
        out_shape=shape(ROWS, WIDE),
        in_specs=[whole] + [far] * 6,
        out_specs=whole,
        name=f"expert_layer_{layer}",
        scratch_shapes=[
            pltpu.VMEM((SLOTS, 2 * HIDDEN), BF),
            pltpu.VMEM((HIDDEN, MODEL), BF),
            pltpu.VMEM((MODEL, 2 * HIDDEN), BF),
            pltpu.VMEM((SLOTS, MODEL), BF),
            pltpu.VMEM((SLOTS, 2 * HIDDEN), BF),
            pltpu.VMEM((SLOTS, MODEL), BF),
            pltpu.SemaphoreType.DMA((4, STEPS)),
        ],
        compiler_params=pltpu.CompilerParams(vmem_limit_bytes=BIG),
        cost_estimate=pl.CostEstimate(
            flops=6 * SLOTS * MODEL * HIDDEN, bytes_accessed=20_000_000, transcendentals=0
        ),
    )


def exchange(packed):
    return lax.all_to_all(
        packed.reshape(EXPERTS, PACK, WIDE), "ep", split_axis=0, concat_axis=0, tiled=True
    ).reshape(ROWS, WIDE)


def swapped(value):
    return lax.ppermute(value, "section", [(0, 1), (1, 0)])


def body(top_grads, expert_ids, route_weights, preacts, w_gate_up, w_down):
    section = lax.axis_index("section")
    ids = expert_ids[0].transpose(0, 2, 1).astype(F32)
    weights = route_weights[0].transpose(0, 2, 1)
    own_meta = jnp.tile(jnp.stack([ids, weights]), (1, 1, 1, 4))
    got_meta = swapped(own_meta)
    own_pre = preacts[0, :, 0]
    own_down, own_up = w_down[0, 0], w_gate_up[0, 0]
    got_down = swapped(own_down)
    got_pre = swapped(lax.dynamic_index_in_dim(own_pre, 1 - section, 0, keepdims=False))
    got_up = swapped(own_up)

    packed = small_call(first_kernel, shape(ROWS, WIDE), "send_first", 300_000_000)(
        own_meta, got_meta, top_grads
    )
    send_zero, gather_one, gather_zero = small_call(
        routes_kernel,
        [shape(3, ROWS, 4 * TOKENS), shape(3, 2 * TOKENS, ROWS), shape(3, 2 * TOKENS, ROWS)],
        "routes",
        1_000_000_000,
    )(own_meta, got_meta)
    arrived = exchange(packed)
    operands = (own_pre, got_pre, own_down, got_down, own_up, got_up)
    answered = expert_call(1)(arrived, *operands)
    returned = exchange(answered)
    lower, packed = small_call(
        relay_kernel, [shape(TOKENS, MODEL), shape(ROWS, WIDE)], "relay", 500_000_000
    )(returned, gather_one, send_zero, top_grads)
    from_zero = lax.ppermute(lower, "section", [(0, 1)])
    arrived = exchange(packed)
    answered = expert_call(0)(arrived, *operands)
    returned = exchange(answered)
    final = small_call(last_kernel, shape(TOKENS, MODEL), "gather_last", 200_000_000)(
        returned, gather_zero, lower
    )
    from_one = lax.ppermute(final, "section", [(1, 0)])
    first = jnp.where(section == 0, final, from_zero)
    second = jnp.where(section == 0, from_one, lower)
    return jnp.stack([first, second])[None]


def solution(mesh):
    placed = (
        P(None, "ep", None),
        P("section", None, "ep", None),
        P("section", None, "ep", None),
        P("section", None, "ep", None, None),
        P("section", "ep", None, None),
        P("section", "ep", None, None),
    )
    return jax.shard_map(
        body, mesh=mesh, in_specs=placed, out_specs=P("section", None, "ep", None), check_vma=False
    )
```

```python
import jax
import jax.numpy as jnp
from jax import lax
from jax.experimental import pallas as pl
from jax.experimental.pallas import tpu as pltpu
from jax.sharding import PartitionSpec as P

alpha_glu = 1.702
BF = jnp.bfloat16
F32 = jnp.float32

MODEL = 1536
HIDDEN = 1536
TOKENS = 64
EXPERTS = 64
TOP = 4
CAP = 6
SLOTS = EXPERTS * CAP
PACK = 8
PART = MODEL // 4
WIDE = 3 * PART
ROWS = EXPERTS * PACK
BLOCKS = 16
GROUP_SLOTS = BLOCKS * CAP
GROUP_ROWS = BLOCKS * PACK
GROUPS = EXPERTS // BLOCKS
TILE = 256
STEPS = HIDDEN // TILE
FIRST_WAITS = 2
SECOND_WAITS = 2
PIECES = 4
BIG = 48 * 1024 * 1024
EXPERT_BIG = 48 * 1024 * 1024


def iota(shape, axis):
    return lax.broadcasted_iota(jnp.int32, shape, axis)


def dot(a, b, contract=((1,), (0,))):
    return lax.dot_general(a, b, (contract, ((), ())), preferred_element_type=F32)


def fetch(own, got, layer, pairs, sem):
    section = lax.axis_index("section")
    held = [to for to, _ in pairs]
    slots = [slot for _, slot in pairs]

    @pl.when(section == layer)
    def _():
        for source, to, slot in zip(own, held, slots):
            pltpu.make_async_copy(source.at[layer], to, sem.at[slot]).start()

    @pl.when(section != layer)
    def _():
        for source, to, slot in zip(got, held, slots):
            pltpu.make_async_copy(source.at[1 - layer], to, sem.at[slot]).start()


def settle(source, to, sem):
    pltpu.make_async_copy(source, to, sem).wait()


def lanes(value, times):
    return jnp.concatenate([value] * times, axis=1)


def named(ids, shape):
    expert = (iota(shape, 0) // PACK).astype(F32)
    return [ids[k : k + 1, :] == expert for k in range(TOP)]


def slot_counts(picked, lanes):
    earlier = (iota((TOKENS, lanes), 0) < (iota((TOKENS, lanes), 1) % TOKENS)).astype(BF)
    return dot(picked.astype(BF), earlier)


def wanted_slots(shape, part):
    row = iota(shape, 0) % PACK
    main = row
    extra = jnp.where(row >= CAP, 3 * (row - CAP) + part, -1)
    return main, extra


def send_masks(ids, weights):
    shape = (ROWS, 4 * TOKENS)
    hits = named(ids, shape)
    weight = jnp.zeros(shape, F32)
    for k in range(TOP):
        weight = weight + jnp.where(hits[k], weights[k : k + 1, :], 0.0)
    picked = hits[0] | hits[1] | hits[2] | hits[3]
    counts = slot_counts(jnp.where(picked, 1.0, 0.0)[:, :TOKENS], 4 * TOKENS)
    counts = jnp.where(picked, counts, -2.0)
    lead = weight.astype(BF).astype(F32)
    group = iota(shape, 1) // TOKENS
    value = jnp.where(group < 2, lead, weight - lead)
    masks = []
    for part in range(3):
        main, extra = wanted_slots(shape, part)
        slot = jnp.where(group % 2 == 0, main, extra).astype(F32)
        masks.append(jnp.where(counts == slot, value, 0.0).astype(BF))
    return masks


def gather_masks(ids):
    shape = (ROWS, 2 * TOKENS)
    hits = named(ids, shape)
    picked = hits[0] | hits[1] | hits[2] | hits[3]
    counts = slot_counts(jnp.where(picked, 1.0, 0.0)[:, :TOKENS], 2 * TOKENS)
    counts = jnp.where(picked, counts, -2.0)
    group = iota(shape, 1) // TOKENS
    masks = []
    for part in range(3):
        main, extra = wanted_slots(shape, part)
        slot = jnp.where(group == 0, main, extra).astype(F32)
        masks.append(jnp.where(counts == slot, 1.0, 0.0))
    return masks


def send_rows(masks, grads, out_ref):
    last = grads[:, WIDE:]
    for part in range(3):
        here = grads[:, part * PART : (part + 1) * PART]
        rows = jnp.concatenate([here, last, here, last], axis=0)
        out_ref[:, part * PART : (part + 1) * PART] = dot(masks[part], rows).astype(BF)


def gather_rows(masks_ref, packed_ref, grads):
    pieces = []
    last = jnp.zeros((TOKENS, PART), F32)
    for part in range(3):
        both = dot(masks_ref[part], packed_ref[:, part * PART : (part + 1) * PART])
        pieces.append(both[:TOKENS])
        last = last + both[TOKENS:]
    total = jnp.concatenate(pieces + [last], axis=1)
    return (grads.astype(F32) + total).astype(BF)


def first_kernel(own_ids, own_w, got_ids, got_w, grads_ref, out_ref, ids, weights, grads, sem):
    section = lax.axis_index("section")
    fetch((own_ids, own_w), (got_ids, got_w), 1, ((ids, 0), (weights, 1)), sem)
    rows = pltpu.make_async_copy(grads_ref.at[section], grads, sem.at[2])
    rows.start()
    settle(own_ids.at[0], ids, sem.at[0])
    settle(own_w.at[0], weights, sem.at[1])
    masks = send_masks(lanes(ids[...].astype(F32), 4), lanes(weights[...], 4))
    rows.wait()
    send_rows(masks, grads[...], out_ref)


def routes_kernel(
    own_ids, own_w, got_ids, got_w, send_ref, gather_one_ref, gather_zero_ref,
    ids_one, ids_zero, weights, sem,
):
    fetch((own_ids,), (got_ids,), 1, ((ids_one, 0),), sem)
    fetch((own_ids, own_w), (got_ids, got_w), 0, ((ids_zero, 1), (weights, 2)), sem)
    settle(own_ids.at[0], ids_one, sem.at[0])
    settle(own_ids.at[0], ids_zero, sem.at[1])
    settle(own_w.at[0], weights, sem.at[2])
    for ids, out in ((ids_one, gather_one_ref), (ids_zero, gather_zero_ref)):
        for part, mask in enumerate(gather_masks(lanes(ids[...].astype(F32), 2))):
            out[part] = mask.T.astype(BF)
    masks = send_masks(lanes(ids_zero[...].astype(F32), 4), lanes(weights[...], 4))
    for part, mask in enumerate(masks):
        send_ref[part] = mask


def other_kernel(pre_ref, out_ref, held, sems):
    section = lax.axis_index("section")
    into, out = [], []
    for piece in range(PIECES):
        here = pl.ds(piece * (SLOTS // PIECES), SLOTS // PIECES)
        into.append(pltpu.make_async_copy(pre_ref.at[1 - section, here], held.at[here], sems.at[0, piece]))
        out.append(pltpu.make_async_copy(held.at[here], out_ref.at[here], sems.at[1, piece]))
    for copy in into:
        copy.start()
    for piece in range(PIECES):
        into[piece].wait()
        out[piece].start()
    for copy in out:
        copy.wait()


def relay_kernel(
    packed_ref, gather_ref, send_ref, grads_ref, lower_ref, out_ref, gather, send, grads, sem
):
    section = lax.axis_index("section")
    copies = [
        pltpu.make_async_copy(gather_ref, gather, sem.at[0]),
        pltpu.make_async_copy(grads_ref.at[section], grads, sem.at[1]),
        pltpu.make_async_copy(send_ref, send, sem.at[2]),
    ]
    for copy in copies:
        copy.start()
    copies[0].wait()
    copies[1].wait()
    lower = gather_rows(gather, packed_ref, grads[...])
    lower_ref[...] = lower
    copies[2].wait()
    send_rows([send[part] for part in range(3)], lower, out_ref)


def last_kernel(packed_ref, gather_ref, grads_ref, out_ref, gather, grads, sem):
    copies = [
        pltpu.make_async_copy(gather_ref, gather, sem.at[0]),
        pltpu.make_async_copy(grads_ref, grads, sem.at[1]),
    ]
    for copy in copies:
        copy.start()
    for copy in copies:
        copy.wait()
    out_ref[...] = gather_rows(gather, packed_ref, grads[...])


def group_masks():
    shape = (GROUP_ROWS, GROUP_SLOTS)
    row, column = iota(shape, 0), iota(shape, 1)
    block = (column * 43) >> 8
    slot = column - CAP * block
    same = (row >> 3) == block
    inner = row & 7
    main = same & (inner == slot)
    extra = [same & (inner >= CAP) & (slot == 3 * (inner - CAP) + part) for part in range(3)]
    return [jnp.where(mask, 1.0, 0.0) for mask in [main] + extra]


def expert_kernel(
    layer, packed_ref, own_pre, got_pre, own_down, got_down, own_up, got_up,
    out_ref, pre, down, up, rows, joined, answers, sems,
):
    section = lax.axis_index("section")

    def copies(step, from_pre, from_down, from_up):
        if step >= STEPS:
            here = pl.ds((step - STEPS) * TILE, TILE)
            return [pltpu.make_async_copy(from_up.at[here], up.at[here], sems.at[0, step])]
        here = pl.ds(step * TILE, TILE)
        there = pl.ds(HIDDEN + step * TILE, TILE)
        return [
            pltpu.make_async_copy(from_down.at[here], down.at[here], sems.at[0, step]),
            pltpu.make_async_copy(from_pre.at[:, here], pre.at[:, here], sems.at[1, step]),
            pltpu.make_async_copy(from_pre.at[:, there], pre.at[:, there], sems.at[2, step]),
        ]

    @pl.when(section == layer)
    def _():
        for step in range(2 * STEPS):
            for copy in copies(step, own_pre.at[layer], own_down, own_up):
                copy.start()

    @pl.when(section != layer)
    def _():
        for step in range(2 * STEPS):
            for copy in copies(step, got_pre, got_down, got_up):
                copy.start()

    def finish(step):
        for copy in copies(step, got_pre, got_down, got_up):
            copy.wait()

    masks = group_masks()
    pack_masks = [
        jnp.concatenate([masks[0], masks[1 + part]], axis=1).astype(BF) for part in range(3)
    ]
    open_main = masks[0].T.astype(BF)
    open_last = jnp.concatenate([masks[1 + part].T for part in range(3)], axis=1).astype(BF)
    for group in range(GROUPS):
        taken = packed_ref[group * GROUP_ROWS : (group + 1) * GROUP_ROWS, :]
        target = slice(group * GROUP_SLOTS, (group + 1) * GROUP_SLOTS)
        rows[target, :WIDE] = dot(open_main, taken).astype(BF)
        stacked = jnp.concatenate(
            [taken[:, part * PART : (part + 1) * PART] for part in range(3)], axis=0
        )
        rows[target, WIDE:] = dot(open_last, stacked).astype(BF)

    for step in range(0, STEPS, FIRST_WAITS):
        here = slice(step * TILE, (step + FIRST_WAITS) * TILE)
        there = slice(HIDDEN + step * TILE, HIDDEN + (step + FIRST_WAITS) * TILE)
        for ready in range(step, step + FIRST_WAITS):
            finish(ready)
        back = dot(rows[...], down[here, :], ((1,), (1,)))
        gate = pre[:, here].astype(F32)
        linear = pre[:, there].astype(F32)
        sigmoid = jax.nn.sigmoid(alpha_glu * gate)
        joined[:, there] = (back * gate * sigmoid).astype(BF)
        joined[:, here] = (
            back * (linear + 1.0) * sigmoid * (1.0 + alpha_glu * gate * (1.0 - sigmoid))
        ).astype(BF)
    for step in range(0, STEPS, SECOND_WAITS):
        here = slice(step * TILE, (step + SECOND_WAITS) * TILE)
        for ready in range(step, step + SECOND_WAITS):
            finish(STEPS + ready)
        answers[:, here] = dot(joined[...], up[here, :], ((1,), (1,))).astype(BF)
    for group in range(GROUPS):
        source = slice(group * GROUP_SLOTS, (group + 1) * GROUP_SLOTS)
        target = slice(group * GROUP_ROWS, (group + 1) * GROUP_ROWS)
        last = answers[source, WIDE:]
        for part in range(3):
            columns = slice(part * PART, (part + 1) * PART)
            both = jnp.concatenate([answers[source, columns], last], axis=0)
            out_ref[target, columns] = dot(pack_masks[part], both).astype(BF)


def shape(*dims, dtype=BF):
    return jax.ShapeDtypeStruct(dims, dtype)


NEAR = pl.BlockSpec(memory_space=pltpu.VMEM)
FAR = pl.BlockSpec(memory_space=pl.ANY)
MASKS = [(3, ROWS, 4 * TOKENS), (3, 2 * TOKENS, ROWS), (3, 2 * TOKENS, ROWS)]


def call_far(ins, call):
    def run(*operands):
        kept = [
            pltpu.with_memory_space_constraint(value, pltpu.MemorySpace.HBM) if spec is FAR else value
            for value, spec in zip(operands, ins)
        ]
        return call(*kept)

    return run


def small_call(kernel, outs, ins, scratch, copies, name, flops, out_specs=NEAR, still=False):
    call = pl.pallas_call(
        kernel,
        out_shape=outs,
        in_specs=ins,
        out_specs=out_specs,
        name=name,
        scratch_shapes=scratch + [pltpu.SemaphoreType.DMA(copies)],
        compiler_params=pltpu.CompilerParams(vmem_limit_bytes=BIG),
        cost_estimate=pl.CostEstimate(flops=flops, bytes_accessed=4_000_000, transcendentals=0),
    )
    return call_far(ins, call) if still else call


def expert_call(layer):
    return pl.pallas_call(
        lambda *refs: expert_kernel(layer, *refs),
        out_shape=shape(ROWS, WIDE),
        in_specs=[NEAR] + [FAR] * 6,
        out_specs=NEAR,
        name=f"expert_layer_{layer}",
        scratch_shapes=[
            pltpu.VMEM((SLOTS, 2 * HIDDEN), BF),
            pltpu.VMEM((HIDDEN, MODEL), BF),
            pltpu.VMEM((MODEL, 2 * HIDDEN), BF),
            pltpu.VMEM((SLOTS, MODEL), BF),
            pltpu.VMEM((SLOTS, 2 * HIDDEN), BF),
            pltpu.VMEM((SLOTS, MODEL), BF),
            pltpu.SemaphoreType.DMA((3, 2 * STEPS)),
        ],
        compiler_params=pltpu.CompilerParams(vmem_limit_bytes=EXPERT_BIG),
        cost_estimate=pl.CostEstimate(
            flops=6 * SLOTS * MODEL * HIDDEN, bytes_accessed=20_000_000, transcendentals=0
        ),
    )


def exchange(packed):
    return lax.all_to_all(
        packed.reshape(EXPERTS, PACK, WIDE), "ep", split_axis=0, concat_axis=0, tiled=True
    ).reshape(ROWS, WIDE)


def swapped(value):
    return lax.ppermute(value, "section", [(0, 1), (1, 0)])


def after(value, *others):
    return lax.optimization_barrier((value,) + others)[0]


def body(top_grads, expert_ids, route_weights, preacts, w_gate_up, w_down):
    section = lax.axis_index("section")
    own_ids = expert_ids[0].transpose(0, 2, 1)
    own_w = route_weights[0].transpose(0, 2, 1)
    own_pre = preacts[0, :, 0]
    own_down, own_up = w_down[0, 0], w_gate_up[0, 0]
    got_ids, got_w = swapped(own_ids), swapped(own_w)
    other_pre = small_call(
        other_kernel,
        shape(SLOTS, 2 * HIDDEN),
        [FAR],
        [pltpu.VMEM((SLOTS, 2 * HIDDEN), BF)],
        (2, PIECES),
        "other_pre",
        1_000_000,
        FAR,
    )(own_pre)
    got_down = swapped(after(own_down, got_ids, got_w))
    got_up = swapped(after(own_up, got_ids, got_w))
    got_pre = swapped(other_pre)

    picks = [pltpu.VMEM((TOP, TOKENS), jnp.int32), pltpu.VMEM((TOP, TOKENS), F32)]
    grads = pltpu.VMEM((TOKENS, MODEL), BF)
    packed = small_call(
        first_kernel, shape(ROWS, WIDE), [FAR] * 5, picks + [grads], (3,), "send_first", 300_000_000
    )(own_ids, own_w, got_ids, got_w, top_grads)
    send_zero, gather_one, gather_zero = small_call(
        routes_kernel,
        [shape(*dims) for dims in MASKS],
        [FAR] * 4,
        picks[:1] + picks,
        (3,),
        "routes",
        1_000_000_000,
        [NEAR] * 3,
    )(own_ids, own_w, after(got_ids, packed), got_w)
    arrived = exchange(packed)
    operands = (own_pre, got_pre, own_down, got_down, own_up, got_up)
    answered = expert_call(1)(arrived, *operands)
    returned = exchange(answered)
    lower, packed = small_call(
        relay_kernel,
        [shape(TOKENS, MODEL), shape(ROWS, WIDE)],
        [NEAR] + [FAR] * 3,
        [pltpu.VMEM(MASKS[1], BF), pltpu.VMEM(MASKS[0], BF), grads],
        (3,),
        "relay",
        500_000_000,
        [NEAR] * 2,
        True,
    )(returned, gather_one, send_zero, top_grads)
    arrived = exchange(packed)
    answered = expert_call(0)(arrived, *operands)
    returned = exchange(answered)
    final = small_call(
        last_kernel,
        shape(TOKENS, MODEL),
        [NEAR] + [FAR] * 2,
        [pltpu.VMEM(MASKS[2], BF), grads],
        (2,),
        "gather_last",
        200_000_000,
        NEAR,
        True,
    )(returned, gather_zero, lower)
    other = swapped(jnp.where(section == 0, lower, final))
    first = jnp.where(section == 0, final, other)
    second = jnp.where(section == 0, other, lower)
    return jnp.stack([first, second])[None]


def solution(mesh):
    placed = (
        P(None, "ep", None),
        P("section", None, "ep", None),
        P("section", None, "ep", None),
        P("section", None, "ep", None, None),
        P("section", "ep", None, None),
        P("section", "ep", None, None),
    )
    return jax.shard_map(
        body, mesh=mesh, in_specs=placed, out_specs=P("section", None, "ep", None), check_vma=False
    )
```

```python
import jax
import jax.numpy as jnp
from jax import lax
from jax.experimental import pallas as pl
from jax.experimental.pallas import tpu as pltpu
from jax.sharding import PartitionSpec as P

alpha_glu = 1.702
BF = jnp.bfloat16
F32 = jnp.float32

MODEL = 1536
HIDDEN = 1536
TOKENS = 64
EXPERTS = 64
TOP = 4
CAP = 6
SLOTS = EXPERTS * CAP
PACK = 8
PART = MODEL // 4
WIDE = 3 * PART
ROWS = EXPERTS * PACK
BLOCKS = 16
GROUP_SLOTS = BLOCKS * CAP
GROUP_ROWS = BLOCKS * PACK
GROUPS = EXPERTS // BLOCKS
TILE = 256
STEPS = HIDDEN // TILE
FIRST_WAITS = 2
SECOND_WAITS = 2
PIECES = 4
BIG = 48 * 1024 * 1024
EXPERT_BIG = 48 * 1024 * 1024


def iota(shape, axis):
    return lax.broadcasted_iota(jnp.int32, shape, axis)


def dot(a, b, contract=((1,), (0,))):
    return lax.dot_general(a, b, (contract, ((), ())), preferred_element_type=F32)


def fetch(own, got, layer, pairs, sem):
    section = lax.axis_index("section")
    held = [to for to, _ in pairs]
    slots = [slot for _, slot in pairs]

    @pl.when(section == layer)
    def _():
        for source, to, slot in zip(own, held, slots):
            pltpu.make_async_copy(source.at[layer], to, sem.at[slot]).start()

    @pl.when(section != layer)
    def _():
        for source, to, slot in zip(got, held, slots):
            pltpu.make_async_copy(source.at[1 - layer], to, sem.at[slot]).start()


def settle(source, to, sem):
    pltpu.make_async_copy(source, to, sem).wait()


def lanes(value, times):
    return jnp.concatenate([value] * times, axis=1)


def named(ids, shape):
    expert = (iota(shape, 0) // PACK).astype(F32)
    return [ids[k : k + 1, :] == expert for k in range(TOP)]


def slot_counts(picked, lanes):
    earlier = (iota((TOKENS, lanes), 0) < (iota((TOKENS, lanes), 1) % TOKENS)).astype(BF)
    return dot(picked.astype(BF), earlier)


def wanted_slots(shape, part):
    row = iota(shape, 0) % PACK
    main = row
    extra = jnp.where(row >= CAP, 3 * (row - CAP) + part, -1)
    return main, extra


def send_masks(ids, weights):
    shape = (ROWS, 4 * TOKENS)
    hits = named(ids, shape)
    weight = jnp.zeros(shape, F32)
    for k in range(TOP):
        weight = weight + jnp.where(hits[k], weights[k : k + 1, :], 0.0)
    picked = hits[0] | hits[1] | hits[2] | hits[3]
    counts = slot_counts(jnp.where(picked, 1.0, 0.0)[:, :TOKENS], 4 * TOKENS)
    counts = jnp.where(picked, counts, -2.0)
    lead = weight.astype(BF).astype(F32)
    group = iota(shape, 1) // TOKENS
    value = jnp.where(group < 2, lead, weight - lead)
    masks = []
    for part in range(3):
        main, extra = wanted_slots(shape, part)
        slot = jnp.where(group % 2 == 0, main, extra).astype(F32)
        masks.append(jnp.where(counts == slot, value, 0.0).astype(BF))
    return masks


def gather_masks(ids):
    shape = (ROWS, 2 * TOKENS)
    hits = named(ids, shape)
    picked = hits[0] | hits[1] | hits[2] | hits[3]
    counts = slot_counts(jnp.where(picked, 1.0, 0.0)[:, :TOKENS], 2 * TOKENS)
    counts = jnp.where(picked, counts, -2.0)
    group = iota(shape, 1) // TOKENS
    masks = []
    for part in range(3):
        main, extra = wanted_slots(shape, part)
        slot = jnp.where(group == 0, main, extra).astype(F32)
        masks.append(jnp.where(counts == slot, 1.0, 0.0))
    return masks


def send_rows(masks, grads, out_ref):
    last = grads[:, WIDE:]
    for part in range(3):
        here = grads[:, part * PART : (part + 1) * PART]
        rows = jnp.concatenate([here, last, here, last], axis=0)
        out_ref[:, part * PART : (part + 1) * PART] = dot(masks[part], rows).astype(BF)


def gather_rows(masks_ref, packed_ref, grads):
    pieces = []
    last = jnp.zeros((TOKENS, PART), F32)
    for part in range(3):
        both = dot(masks_ref[part], packed_ref[:, part * PART : (part + 1) * PART])
        pieces.append(both[:TOKENS])
        last = last + both[TOKENS:]
    total = jnp.concatenate(pieces + [last], axis=1)
    return (grads.astype(F32) + total).astype(BF)


def first_kernel(own_ids, own_w, got_ids, got_w, grads_ref, out_ref, ids, weights, grads, sem):
    section = lax.axis_index("section")
    fetch((own_ids, own_w), (got_ids, got_w), 1, ((ids, 0), (weights, 1)), sem)
    rows = pltpu.make_async_copy(grads_ref.at[section], grads, sem.at[2])
    rows.start()
    settle(own_ids.at[0], ids, sem.at[0])
    settle(own_w.at[0], weights, sem.at[1])
    masks = send_masks(lanes(ids[...].astype(F32), 4), lanes(weights[...], 4))
    rows.wait()
    send_rows(masks, grads[...], out_ref)


def other_kernel(pre_ref, out_ref, sems):
    section = lax.axis_index("section")
    copies = []
    for piece in range(PIECES):
        here = pl.ds(piece * (SLOTS // PIECES), SLOTS // PIECES)
        copies.append(
            pltpu.make_async_copy(pre_ref.at[1 - section, here], out_ref.at[here], sems.at[piece])
        )
    for copy in copies:
        copy.start()
    for copy in copies:
        copy.wait()


def factors(gate, linear):
    sigmoid = jax.nn.sigmoid(alpha_glu * gate)
    for_gate = (linear + 1.0) * sigmoid * (1.0 + alpha_glu * gate * (1.0 - sigmoid))
    return for_gate, gate * sigmoid


def factors_kernel(pre_ref, first_ref, second_ref, held, made, sems):
    working = lax.axis_index("section") == 0
    size = SLOTS // PIECES
    pieces = [(micro, piece) for micro in (0, 1) for piece in range(PIECES)]

    def into(micro, piece):
        here = pl.ds(piece * size, size)
        return pltpu.make_async_copy(
            pre_ref.at[micro, here], held.at[micro, here], sems.at[0, micro, piece]
        )

    def out(micro, piece):
        here = pl.ds(piece * size, size)
        target = (first_ref, second_ref)[micro]
        return pltpu.make_async_copy(made.at[micro, here], target.at[here], sems.at[1, micro, piece])

    @pl.when(working)
    def _():
        for micro, piece in pieces:
            into(micro, piece).start()

    @pl.when(working)
    def _():
        for micro, piece in pieces:
            into(micro, piece).wait()
            here = slice(piece * size, (piece + 1) * size)
            for_gate, for_up = factors(
                held[micro, here, :HIDDEN].astype(F32), held[micro, here, HIDDEN:].astype(F32)
            )
            made[micro, here, :HIDDEN] = for_gate.astype(BF)
            made[micro, here, HIDDEN:] = for_up.astype(BF)
            out(micro, piece).start()
        for micro, piece in pieces:
            out(micro, piece).wait()


def routes_kernel(mine, own_ids, own_w, got_ids, got_w, *refs):
    outs = refs[-10:-7]
    ids_one, ids_zero, weights, send, gather_one, gather_zero, sem = refs[-7:]
    working = lax.axis_index("section") == mine
    one = got_ids if mine == 0 else own_ids
    ids, w = (own_ids, own_w) if mine == 0 else (got_ids, got_w)
    picks = [
        pltpu.make_async_copy(one.at[mine], ids_one, sem.at[0]),
        pltpu.make_async_copy(ids.at[mine], ids_zero, sem.at[1]),
        pltpu.make_async_copy(w.at[mine], weights, sem.at[2]),
    ]
    masks_out = [
        pltpu.make_async_copy(value, target, sem.at[3 + place])
        for place, (value, target) in enumerate(zip((send, gather_one, gather_zero), outs))
    ]

    @pl.when(working)
    def _():
        for copy in picks:
            copy.start()
        for copy in picks:
            copy.wait()
        for ids_held, target in ((ids_one, gather_one), (ids_zero, gather_zero)):
            for part, mask in enumerate(gather_masks(lanes(ids_held[...].astype(F32), 2))):
                target[part] = mask.T.astype(BF)
        masks = send_masks(lanes(ids_zero[...].astype(F32), 4), lanes(weights[...], 4))
        for part, mask in enumerate(masks):
            send[part] = mask
        for copy in masks_out:
            copy.start()
        for copy in masks_out:
            copy.wait()


def relay_kernel(
    packed_ref, gather_ref, send_ref, grads_ref, lower_ref, out_ref, gather, send, grads, sem
):
    section = lax.axis_index("section")
    copies = [
        pltpu.make_async_copy(gather_ref, gather, sem.at[0]),
        pltpu.make_async_copy(grads_ref.at[section], grads, sem.at[1]),
        pltpu.make_async_copy(send_ref, send, sem.at[2]),
    ]
    for copy in copies:
        copy.start()
    copies[0].wait()
    copies[1].wait()
    lower = gather_rows(gather, packed_ref, grads[...])
    lower_ref[...] = lower
    copies[2].wait()
    send_rows([send[part] for part in range(3)], lower, out_ref)


def last_kernel(packed_ref, gather_ref, grads_ref, out_ref, gather, grads, sem):
    copies = [
        pltpu.make_async_copy(gather_ref, gather, sem.at[0]),
        pltpu.make_async_copy(grads_ref, grads, sem.at[1]),
    ]
    for copy in copies:
        copy.start()
    for copy in copies:
        copy.wait()
    out_ref[...] = gather_rows(gather, packed_ref, grads[...])


def group_masks():
    shape = (GROUP_ROWS, GROUP_SLOTS)
    row, column = iota(shape, 0), iota(shape, 1)
    block = (column * 43) >> 8
    slot = column - CAP * block
    same = (row >> 3) == block
    inner = row & 7
    main = same & (inner == slot)
    extra = [same & (inner >= CAP) & (slot == 3 * (inner - CAP) + part) for part in range(3)]
    return [jnp.where(mask, 1.0, 0.0) for mask in [main] + extra]


def expert_kernel(
    layer, packed_ref, own_pre, got_pre, own_down, got_down, own_up, got_up,
    out_ref, pre, down, up, rows, joined, answers, sems,
):
    section = lax.axis_index("section")

    def copies(step, from_pre, from_down, from_up):
        if step >= STEPS:
            here = pl.ds((step - STEPS) * TILE, TILE)
            return [pltpu.make_async_copy(from_up.at[here], up.at[here], sems.at[0, step])]
        here = pl.ds(step * TILE, TILE)
        there = pl.ds(HIDDEN + step * TILE, TILE)
        return [
            pltpu.make_async_copy(from_down.at[here], down.at[here], sems.at[0, step]),
            pltpu.make_async_copy(from_pre.at[:, here], pre.at[:, here], sems.at[1, step]),
            pltpu.make_async_copy(from_pre.at[:, there], pre.at[:, there], sems.at[2, step]),
        ]

    @pl.when(section == layer)
    def _():
        for step in range(2 * STEPS):
            for copy in copies(step, own_pre.at[1] if layer else own_pre, own_down, own_up):
                copy.start()

    @pl.when(section != layer)
    def _():
        for step in range(2 * STEPS):
            for copy in copies(step, got_pre, got_down, got_up):
                copy.start()

    def finish(step):
        for copy in copies(step, got_pre, got_down, got_up):
            copy.wait()

    masks = group_masks()
    pack_masks = [
        jnp.concatenate([masks[0], masks[1 + part]], axis=1).astype(BF) for part in range(3)
    ]
    open_main = masks[0].T.astype(BF)
    open_last = jnp.concatenate([masks[1 + part].T for part in range(3)], axis=1).astype(BF)
    for group in range(GROUPS):
        taken = packed_ref[group * GROUP_ROWS : (group + 1) * GROUP_ROWS, :]
        target = slice(group * GROUP_SLOTS, (group + 1) * GROUP_SLOTS)
        rows[target, :WIDE] = dot(open_main, taken).astype(BF)
        stacked = jnp.concatenate(
            [taken[:, part * PART : (part + 1) * PART] for part in range(3)], axis=0
        )
        rows[target, WIDE:] = dot(open_last, stacked).astype(BF)

    for step in range(0, STEPS, FIRST_WAITS):
        here = slice(step * TILE, (step + FIRST_WAITS) * TILE)
        there = slice(HIDDEN + step * TILE, HIDDEN + (step + FIRST_WAITS) * TILE)
        for ready in range(step, step + FIRST_WAITS):
            finish(ready)
        back = dot(rows[...], down[here, :], ((1,), (1,)))
        for_gate, for_up = pre[:, here].astype(F32), pre[:, there].astype(F32)
        if layer == 1:
            for_gate, for_up = factors(for_gate, for_up)
        joined[:, here] = (back * for_gate).astype(BF)
        joined[:, there] = (back * for_up).astype(BF)
    for step in range(0, STEPS, SECOND_WAITS):
        here = slice(step * TILE, (step + SECOND_WAITS) * TILE)
        for ready in range(step, step + SECOND_WAITS):
            finish(STEPS + ready)
        answers[:, here] = dot(joined[...], up[here, :], ((1,), (1,))).astype(BF)
    for group in range(GROUPS):
        source = slice(group * GROUP_SLOTS, (group + 1) * GROUP_SLOTS)
        target = slice(group * GROUP_ROWS, (group + 1) * GROUP_ROWS)
        last = answers[source, WIDE:]
        for part in range(3):
            columns = slice(part * PART, (part + 1) * PART)
            both = jnp.concatenate([answers[source, columns], last], axis=0)
            out_ref[target, columns] = dot(pack_masks[part], both).astype(BF)


def shape(*dims, dtype=BF):
    return jax.ShapeDtypeStruct(dims, dtype)


NEAR = pl.BlockSpec(memory_space=pltpu.VMEM)
FAR = pl.BlockSpec(memory_space=pl.ANY)
PICK_IDS = pltpu.VMEM((TOP, TOKENS), jnp.int32)
PICK_WEIGHTS = pltpu.VMEM((TOP, TOKENS), F32)
MASKS = [(3, ROWS, 4 * TOKENS), (3, 2 * TOKENS, ROWS), (3, 2 * TOKENS, ROWS)]


def call_far(ins, call):
    def run(*operands):
        kept = [
            pltpu.with_memory_space_constraint(value, pltpu.MemorySpace.HBM) if spec is FAR else value
            for value, spec in zip(operands, ins)
        ]
        return call(*kept)

    return run


def small_call(
    kernel, outs, ins, scratch, copies, name, flops, out_specs=NEAR, still=False, limit=BIG, aliases={},
    cost=4_000_000,
):
    call = pl.pallas_call(
        kernel,
        out_shape=outs,
        in_specs=ins,
        out_specs=out_specs,
        name=name,
        input_output_aliases=aliases,
        scratch_shapes=scratch + [pltpu.SemaphoreType.DMA(copies)],
        compiler_params=pltpu.CompilerParams(vmem_limit_bytes=limit),
        cost_estimate=pl.CostEstimate(flops=flops, bytes_accessed=cost, transcendentals=0),
    )
    return call_far(ins, call) if still else call


def factors_call(pre):
    return small_call(
        factors_kernel,
        [pltpu.HBM((SLOTS, 2 * HIDDEN), BF)] * 2,
        [FAR],
        [pltpu.VMEM((2, SLOTS, 2 * HIDDEN), BF)] * 2,
        (2, 2, PIECES),
        "lower_factors",
        20_000_000,
        [FAR] * 2,
    )(pre)


def routes_call(mine, *operands):
    return small_call(
        lambda *refs: routes_kernel(mine, *refs),
        [pltpu.HBM(dims, BF) for dims in MASKS],
        [FAR] * len(operands),
        [PICK_IDS, PICK_IDS, PICK_WEIGHTS] + [pltpu.VMEM(dims, BF) for dims in MASKS],
        (6,),
        f"routes_section_{mine}",
        1_000_000_000,
        [FAR] * 3,
        aliases={4 + place: place for place in range(len(operands) - 4)},
    )(*operands)


def expert_call(layer):
    return pl.pallas_call(
        lambda *refs: expert_kernel(layer, *refs),
        out_shape=shape(ROWS, WIDE),
        in_specs=[NEAR] + [FAR] * 6,
        out_specs=NEAR,
        name=f"expert_layer_{layer}",
        scratch_shapes=[
            pltpu.VMEM((SLOTS, 2 * HIDDEN), BF),
            pltpu.VMEM((HIDDEN, MODEL), BF),
            pltpu.VMEM((MODEL, 2 * HIDDEN), BF),
            pltpu.VMEM((SLOTS, MODEL), BF),
            pltpu.VMEM((SLOTS, 2 * HIDDEN), BF),
            pltpu.VMEM((SLOTS, MODEL), BF),
            pltpu.SemaphoreType.DMA((3, 2 * STEPS)),
        ],
        compiler_params=pltpu.CompilerParams(vmem_limit_bytes=EXPERT_BIG),
        cost_estimate=pl.CostEstimate(
            flops=6 * SLOTS * MODEL * HIDDEN, bytes_accessed=20_000_000, transcendentals=0
        ),
    )


def exchange(packed):
    return lax.all_to_all(
        packed.reshape(EXPERTS, PACK, WIDE), "ep", split_axis=0, concat_axis=0, tiled=True
    ).reshape(ROWS, WIDE)


def swapped(value):
    return lax.ppermute(value, "section", [(0, 1), (1, 0)])


def after(value, *others):
    return lax.optimization_barrier((value,) + others)[0]


def after_all(values, *others):
    return lax.optimization_barrier(tuple(values) + others)[: len(values)]


def body(top_grads, expert_ids, route_weights, preacts, w_gate_up, w_down):
    section = lax.axis_index("section")
    own_ids = expert_ids[0].transpose(0, 2, 1)
    own_w = route_weights[0].transpose(0, 2, 1)
    own_pre = preacts[0, :, 0]
    own_down, own_up = w_down[0, 0], w_gate_up[0, 0]
    got_ids, got_w = swapped(own_ids), swapped(own_w)
    other_pre = small_call(
        other_kernel, shape(SLOTS, 2 * HIDDEN), [FAR], [], (PIECES,), "other_pre", 1_000_000
    )(own_pre)
    got_down = swapped(after(own_down, got_ids, got_w))
    got_up = swapped(after(own_up, got_ids, got_w))
    got_pre = swapped(other_pre)
    picks = (own_ids, own_w, got_ids, got_w)

    own_factors, other_factors = factors_call(after(own_pre, got_ids, got_w, other_pre))
    masks = routes_call(0, own_ids, own_w, after(got_ids, own_factors), got_w)

    grads = pltpu.VMEM((TOKENS, MODEL), BF)
    packed = small_call(
        first_kernel,
        shape(ROWS, WIDE),
        [FAR] * 5,
        [PICK_IDS, PICK_WEIGHTS, grads],
        (3,),
        "send_first",
        300_000_000,
    )(own_ids, own_w, after(got_ids, *masks), got_w, top_grads)
    arrived = exchange(packed)
    weights = (own_down, got_down, own_up, got_up)
    answered = expert_call(1)(arrived, own_pre, got_pre, *weights)
    got_factors = lax.ppermute(after(other_factors, answered), "section", [(0, 1)])
    send_zero, gather_one, gather_zero = routes_call(1, *picks, *after_all(masks, answered))
    returned = exchange(answered)
    lower, packed = small_call(
        relay_kernel,
        [shape(TOKENS, MODEL), shape(ROWS, WIDE)],
        [NEAR] + [FAR] * 3,
        [pltpu.VMEM(MASKS[1], BF), pltpu.VMEM(MASKS[0], BF), grads],
        (3,),
        "relay",
        500_000_000,
        [NEAR] * 2,
        True,
    )(returned, gather_one, send_zero, top_grads)
    arrived = exchange(packed)
    answered = expert_call(0)(arrived, own_factors, got_factors, *weights)
    returned = exchange(answered)
    final = small_call(
        last_kernel,
        shape(TOKENS, MODEL),
        [NEAR] + [FAR] * 2,
        [pltpu.VMEM(MASKS[2], BF), grads],
        (2,),
        "gather_last",
        200_000_000,
        NEAR,
        True,
    )(returned, gather_zero, lower)
    other = swapped(jnp.where(section == 0, lower, final))
    first = jnp.where(section == 0, final, other)
    second = jnp.where(section == 0, other, lower)
    return jnp.stack([first, second])[None]


def solution(mesh):
    placed = (
        P(None, "ep", None),
        P("section", None, "ep", None),
        P("section", None, "ep", None),
        P("section", None, "ep", None, None),
        P("section", "ep", None, None),
        P("section", "ep", None, None),
    )
    return jax.shard_map(
        body, mesh=mesh, in_specs=placed, out_specs=P("section", None, "ep", None), check_vma=False
    )
```

```python
import jax
import jax.numpy as jnp
from jax import lax
from jax.experimental import pallas as pl
from jax.experimental.pallas import tpu as pltpu
from jax.sharding import PartitionSpec as P

alpha_glu = 1.702
BF = jnp.bfloat16
F32 = jnp.float32

MODEL = 1536
HIDDEN = 1536
TOKENS = 64
EXPERTS = 64
TOP = 4
CAP = 6
SLOTS = EXPERTS * CAP
PACK = 8
PART = MODEL // 4
WIDE = 3 * PART
ROWS = EXPERTS * PACK
BLOCKS = 16
GROUP_SLOTS = BLOCKS * CAP
GROUP_ROWS = BLOCKS * PACK
GROUPS = EXPERTS // BLOCKS
TILE = 256
STEPS = HIDDEN // TILE
FIRST_WAITS = 2
SECOND_WAITS = 2
PIECES = 4
BIG = 48 * 1024 * 1024
EXPERT_BIG = 48 * 1024 * 1024
SMALL = 16 * 1024 * 1024


def iota(shape, axis):
    return lax.broadcasted_iota(jnp.int32, shape, axis)


def dot(a, b, contract=((1,), (0,))):
    return lax.dot_general(a, b, (contract, ((), ())), preferred_element_type=F32)


def fetch(own, got, layer, pairs, sem):
    section = lax.axis_index("section")
    held = [to for to, _ in pairs]
    slots = [slot for _, slot in pairs]

    @pl.when(section == layer)
    def _():
        for source, to, slot in zip(own, held, slots):
            pltpu.make_async_copy(source.at[layer], to, sem.at[slot]).start()

    @pl.when(section != layer)
    def _():
        for source, to, slot in zip(got, held, slots):
            pltpu.make_async_copy(source.at[1 - layer], to, sem.at[slot]).start()


def settle(source, to, sem):
    pltpu.make_async_copy(source, to, sem).wait()


def lanes(value, times):
    return jnp.concatenate([value] * times, axis=1)


def named(ids, shape):
    expert = (iota(shape, 0) // PACK).astype(F32)
    return [ids[k : k + 1, :] == expert for k in range(TOP)]


def slot_counts(picked, lanes):
    earlier = (iota((TOKENS, lanes), 0) < (iota((TOKENS, lanes), 1) % TOKENS)).astype(BF)
    return dot(picked.astype(BF), earlier)


def wanted_slots(shape, part):
    row = iota(shape, 0) % PACK
    main = row
    extra = jnp.where(row >= CAP, 3 * (row - CAP) + part, -1)
    return main, extra


def send_masks(ids, weights):
    shape = (ROWS, 4 * TOKENS)
    hits = named(ids, shape)
    weight = jnp.zeros(shape, F32)
    for k in range(TOP):
        weight = weight + jnp.where(hits[k], weights[k : k + 1, :], 0.0)
    picked = hits[0] | hits[1] | hits[2] | hits[3]
    counts = slot_counts(jnp.where(picked, 1.0, 0.0)[:, :TOKENS], 4 * TOKENS)
    counts = jnp.where(picked, counts, -2.0)
    lead = weight.astype(BF).astype(F32)
    group = iota(shape, 1) // TOKENS
    value = jnp.where(group < 2, lead, weight - lead)
    masks = []
    for part in range(3):
        main, extra = wanted_slots(shape, part)
        slot = jnp.where(group % 2 == 0, main, extra).astype(F32)
        masks.append(jnp.where(counts == slot, value, 0.0).astype(BF))
    return masks


def gather_masks(ids):
    shape = (ROWS, 2 * TOKENS)
    hits = named(ids, shape)
    picked = hits[0] | hits[1] | hits[2] | hits[3]
    counts = slot_counts(jnp.where(picked, 1.0, 0.0)[:, :TOKENS], 2 * TOKENS)
    counts = jnp.where(picked, counts, -2.0)
    group = iota(shape, 1) // TOKENS
    masks = []
    for part in range(3):
        main, extra = wanted_slots(shape, part)
        slot = jnp.where(group == 0, main, extra).astype(F32)
        masks.append(jnp.where(counts == slot, 1.0, 0.0))
    return masks


def send_rows(masks, grads, out_ref):
    last = grads[:, WIDE:]
    for part in range(3):
        here = grads[:, part * PART : (part + 1) * PART]
        rows = jnp.concatenate([here, last, here, last], axis=0)
        out_ref[:, part * PART : (part + 1) * PART] = dot(masks[part], rows).astype(BF)


def gather_rows(masks_ref, packed_ref, grads):
    pieces = []
    last = jnp.zeros((TOKENS, PART), F32)
    for part in range(3):
        both = dot(masks_ref[part], packed_ref[:, part * PART : (part + 1) * PART])
        pieces.append(both[:TOKENS])
        last = last + both[TOKENS:]
    total = jnp.concatenate(pieces + [last], axis=1)
    return (grads.astype(F32) + total).astype(BF)


def first_kernel(own_ids, own_w, got_ids, got_w, grads_ref, out_ref, grads, ids, weights, sem):
    section = lax.axis_index("section")
    fetch((own_ids, own_w), (got_ids, got_w), 1, ((ids, 0), (weights, 1)), sem)
    rows = pltpu.make_async_copy(grads_ref.at[section], grads, sem.at[2])
    rows.start()
    settle(own_ids.at[0], ids, sem.at[0])
    settle(own_w.at[0], weights, sem.at[1])
    masks = send_masks(lanes(ids[...].astype(F32), 4), lanes(weights[...], 4))
    rows.wait()
    send_rows(masks, grads[...], out_ref)


def other_kernel(pre_ref, out_ref, sems):
    section = lax.axis_index("section")
    copies = []
    for piece in range(PIECES):
        here = pl.ds(piece * (SLOTS // PIECES), SLOTS // PIECES)
        copies.append(
            pltpu.make_async_copy(pre_ref.at[1 - section, here], out_ref.at[here], sems.at[piece])
        )
    for copy in copies:
        copy.start()
    for copy in copies:
        copy.wait()


def factors(gate, linear):
    sigmoid = jax.nn.sigmoid(alpha_glu * gate)
    for_gate = (linear + 1.0) * sigmoid * (1.0 + alpha_glu * gate * (1.0 - sigmoid))
    return for_gate, gate * sigmoid


def factors_kernel(pre_ref, first_ref, second_ref, held, made, sems):
    working = lax.axis_index("section") == 0
    size = SLOTS // PIECES
    pieces = [(micro, piece) for micro in (0, 1) for piece in range(PIECES)]

    def into(micro, piece):
        here = pl.ds(piece * size, size)
        return pltpu.make_async_copy(
            pre_ref.at[micro, here], held.at[micro, here], sems.at[0, micro, piece]
        )

    def out(micro, piece):
        here = pl.ds(piece * size, size)
        target = (first_ref, second_ref)[micro]
        return pltpu.make_async_copy(made.at[micro, here], target.at[here], sems.at[1, micro, piece])

    @pl.when(working)
    def _():
        for micro, piece in pieces:
            into(micro, piece).start()

    @pl.when(working)
    def _():
        for micro, piece in pieces:
            into(micro, piece).wait()
            here = slice(piece * size, (piece + 1) * size)
            for_gate, for_up = factors(
                held[micro, here, :HIDDEN].astype(F32), held[micro, here, HIDDEN:].astype(F32)
            )
            made[micro, here, :HIDDEN] = for_gate.astype(BF)
            made[micro, here, HIDDEN:] = for_up.astype(BF)
            out(micro, piece).start()
        for micro, piece in pieces:
            out(micro, piece).wait()


def routes_kernel(mine, own_ids, own_w, got_ids, got_w, *refs):
    send, gather_one, gather_zero, ids_one, ids_zero, weights, sem = refs[-7:]
    one = got_ids if mine == 0 else own_ids
    ids, w = (own_ids, own_w) if mine == 0 else (got_ids, got_w)

    @pl.when(lax.axis_index("section") == mine)
    def _():
        picks = [
            pltpu.make_async_copy(one.at[mine], ids_one, sem.at[0]),
            pltpu.make_async_copy(ids.at[mine], ids_zero, sem.at[1]),
            pltpu.make_async_copy(w.at[mine], weights, sem.at[2]),
        ]
        for copy in picks:
            copy.start()
        for copy in picks:
            copy.wait()
        for ids_held, target in ((ids_one, gather_one), (ids_zero, gather_zero)):
            for part, mask in enumerate(gather_masks(lanes(ids_held[...].astype(F32), 2))):
                target[part] = mask.T.astype(BF)
        masks = send_masks(lanes(ids_zero[...].astype(F32), 4), lanes(weights[...], 4))
        for part, mask in enumerate(masks):
            send[part] = mask


def relay_kernel(packed_ref, gather, send, grads, lower_ref, out_ref):
    lower = gather_rows(gather, packed_ref, grads[...])
    lower_ref[...] = lower
    send_rows([send[part] for part in range(3)], lower, out_ref)


def last_kernel(packed_ref, gather, grads_ref, out_ref):
    out_ref[...] = gather_rows(gather, packed_ref, grads_ref[...])


def group_masks():
    shape = (GROUP_ROWS, GROUP_SLOTS)
    row, column = iota(shape, 0), iota(shape, 1)
    block = (column * 43) >> 8
    slot = column - CAP * block
    same = (row >> 3) == block
    inner = row & 7
    main = same & (inner == slot)
    extra = [same & (inner >= CAP) & (slot == 3 * (inner - CAP) + part) for part in range(3)]
    return [jnp.where(mask, 1.0, 0.0) for mask in [main] + extra]


def expert_kernel(
    layer, packed_ref, own_pre, got_pre, own_down, got_down, own_up, got_up,
    out_ref, pre, down, up, rows, joined, answers, sems,
):
    section = lax.axis_index("section")

    def copies(step, from_pre, from_down, from_up):
        if step >= STEPS:
            here = pl.ds((step - STEPS) * TILE, TILE)
            return [pltpu.make_async_copy(from_up.at[here], up.at[here], sems.at[0, step])]
        here = pl.ds(step * TILE, TILE)
        there = pl.ds(HIDDEN + step * TILE, TILE)
        return [
            pltpu.make_async_copy(from_down.at[here], down.at[here], sems.at[0, step]),
            pltpu.make_async_copy(from_pre.at[:, here], pre.at[:, here], sems.at[1, step]),
            pltpu.make_async_copy(from_pre.at[:, there], pre.at[:, there], sems.at[2, step]),
        ]

    @pl.when(section == layer)
    def _():
        for step in range(2 * STEPS):
            for copy in copies(step, own_pre.at[1] if layer else own_pre, own_down, own_up):
                copy.start()

    @pl.when(section != layer)
    def _():
        for step in range(2 * STEPS):
            for copy in copies(step, got_pre, got_down, got_up):
                copy.start()

    def finish(step):
        for copy in copies(step, got_pre, got_down, got_up):
            copy.wait()

    masks = group_masks()
    pack_masks = [
        jnp.concatenate([masks[0], masks[1 + part]], axis=1).astype(BF) for part in range(3)
    ]
    open_main = masks[0].T.astype(BF)
    open_last = jnp.concatenate([masks[1 + part].T for part in range(3)], axis=1).astype(BF)
    for group in range(GROUPS):
        taken = packed_ref[group * GROUP_ROWS : (group + 1) * GROUP_ROWS, :]
        target = slice(group * GROUP_SLOTS, (group + 1) * GROUP_SLOTS)
        rows[target, :WIDE] = dot(open_main, taken).astype(BF)
        stacked = jnp.concatenate(
            [taken[:, part * PART : (part + 1) * PART] for part in range(3)], axis=0
        )
        rows[target, WIDE:] = dot(open_last, stacked).astype(BF)

    for step in range(0, STEPS, FIRST_WAITS):
        here = slice(step * TILE, (step + FIRST_WAITS) * TILE)
        there = slice(HIDDEN + step * TILE, HIDDEN + (step + FIRST_WAITS) * TILE)
        for ready in range(step, step + FIRST_WAITS):
            finish(ready)
        back = dot(rows[...], down[here, :], ((1,), (1,)))
        for_gate, for_up = pre[:, here].astype(F32), pre[:, there].astype(F32)
        if layer == 1:
            for_gate, for_up = factors(for_gate, for_up)
        joined[:, here] = (back * for_gate).astype(BF)
        joined[:, there] = (back * for_up).astype(BF)
    for step in range(0, STEPS, SECOND_WAITS):
        here = slice(step * TILE, (step + SECOND_WAITS) * TILE)
        for ready in range(step, step + SECOND_WAITS):
            finish(STEPS + ready)
        answers[:, here] = dot(joined[...], up[here, :], ((1,), (1,))).astype(BF)
    for group in range(GROUPS):
        source = slice(group * GROUP_SLOTS, (group + 1) * GROUP_SLOTS)
        target = slice(group * GROUP_ROWS, (group + 1) * GROUP_ROWS)
        last = answers[source, WIDE:]
        for part in range(3):
            columns = slice(part * PART, (part + 1) * PART)
            both = jnp.concatenate([answers[source, columns], last], axis=0)
            out_ref[target, columns] = dot(pack_masks[part], both).astype(BF)


def shape(*dims, dtype=BF):
    return jax.ShapeDtypeStruct(dims, dtype)


NEAR = pl.BlockSpec(memory_space=pltpu.VMEM)
FAR = pl.BlockSpec(memory_space=pl.ANY)
PICK_IDS = pltpu.VMEM((TOP, TOKENS), jnp.int32)
PICK_WEIGHTS = pltpu.VMEM((TOP, TOKENS), F32)
KEPT = pltpu.VMEM((TOKENS, MODEL), BF)
MASKS = [(3, ROWS, 4 * TOKENS), (3, 2 * TOKENS, ROWS), (3, 2 * TOKENS, ROWS)]


def pinned(value, space):
    return pltpu.with_memory_space_constraint(value, space)


def in_hbm(value):
    return pinned(value, pltpu.MemorySpace.HBM)


def in_vmem(value):
    return pinned(value, pltpu.MemorySpace.VMEM)


def small_call(
    kernel, outs, ins, scratch, copies, name, flops, out_specs=NEAR, limit=BIG, aliases={}, cost=4_000_000
):
    sems = [pltpu.SemaphoreType.DMA(copies)] if copies else []
    return pl.pallas_call(
        kernel,
        out_shape=outs,
        in_specs=ins,
        out_specs=out_specs,
        name=name,
        input_output_aliases=aliases,
        scratch_shapes=scratch + sems,
        compiler_params=pltpu.CompilerParams(vmem_limit_bytes=limit),
        cost_estimate=pl.CostEstimate(flops=flops, bytes_accessed=cost, transcendentals=0),
    )


def factors_call(pre):
    return small_call(
        factors_kernel,
        [pltpu.HBM((SLOTS, 2 * HIDDEN), BF)] * 2,
        [FAR],
        [pltpu.VMEM((2, SLOTS, 2 * HIDDEN), BF)] * 2,
        (2, 2, PIECES),
        "lower_factors",
        20_000_000,
        [FAR] * 2,
    )(pre)


def routes_call(mine, picks, masks):
    return small_call(
        lambda *refs: routes_kernel(mine, *refs),
        [pltpu.VMEM(dims, BF) for dims in MASKS],
        [FAR] * 4 + [NEAR] * len(masks),
        [PICK_IDS, PICK_IDS, PICK_WEIGHTS],
        (3,),
        f"routes_section_{mine}",
        1_000_000_000,
        [NEAR] * 3,
        limit=SMALL,
        aliases={4 + place: place for place in range(len(masks))},
    )(*picks, *[in_vmem(mask) for mask in masks])


def expert_call(layer, *operands):
    return pl.pallas_call(
        lambda *refs: expert_kernel(layer, *refs),
        out_shape=shape(ROWS, WIDE),
        in_specs=[NEAR] + [FAR] * 6,
        out_specs=NEAR,
        name=f"expert_layer_{layer}",
        scratch_shapes=[
            pltpu.VMEM((SLOTS, 2 * HIDDEN), BF),
            pltpu.VMEM((HIDDEN, MODEL), BF),
            pltpu.VMEM((MODEL, 2 * HIDDEN), BF),
            pltpu.VMEM((SLOTS, MODEL), BF),
            pltpu.VMEM((SLOTS, 2 * HIDDEN), BF),
            pltpu.VMEM((SLOTS, MODEL), BF),
            pltpu.SemaphoreType.DMA((3, 2 * STEPS)),
        ],
        compiler_params=pltpu.CompilerParams(vmem_limit_bytes=EXPERT_BIG),
        cost_estimate=pl.CostEstimate(
            flops=6 * SLOTS * MODEL * HIDDEN, bytes_accessed=20_000_000, transcendentals=0
        ),
    )(*operands)


def exchange(packed):
    return lax.all_to_all(
        packed.reshape(EXPERTS, PACK, WIDE), "ep", split_axis=0, concat_axis=0, tiled=True
    ).reshape(ROWS, WIDE)


def swapped(value):
    return lax.ppermute(value, "section", [(0, 1), (1, 0)])


def after(value, *others):
    return lax.optimization_barrier((value,) + others)[0]


def after_all(values, *others):
    return lax.optimization_barrier(tuple(values) + others)[: len(values)]


def body(top_grads, expert_ids, route_weights, preacts, w_gate_up, w_down):
    section = lax.axis_index("section")
    own_ids = expert_ids[0].transpose(0, 2, 1)
    own_w = route_weights[0].transpose(0, 2, 1)
    own_pre = preacts[0, :, 0]
    own_down, own_up = w_down[0, 0], w_gate_up[0, 0]
    got_ids, got_w = swapped(own_ids), swapped(own_w)
    other_pre = small_call(
        other_kernel, shape(SLOTS, 2 * HIDDEN), [FAR], [], (PIECES,), "other_pre", 1_000_000
    )(own_pre)
    got_down = swapped(after(own_down, got_ids, got_w))
    got_up = swapped(after(own_up, got_ids, got_w))
    got_pre = swapped(other_pre)
    picks = (own_ids, own_w, got_ids, got_w)

    own_factors, other_factors = factors_call(after(own_pre, got_ids, got_w, other_pre))
    masks = routes_call(0, (own_ids, own_w, after(got_ids, own_factors), got_w), ())

    packed, grads = small_call(
        first_kernel,
        [shape(ROWS, WIDE), KEPT],
        [FAR] * 5,
        [PICK_IDS, PICK_WEIGHTS],
        (3,),
        "send_first",
        300_000_000,
        [NEAR] * 2,
        limit=SMALL,
    )(own_ids, own_w, after(got_ids, *masks), got_w, in_hbm(top_grads))
    weights = (own_down, got_down, own_up, got_up)
    arrived = exchange(packed)
    answered = expert_call(1, arrived, own_pre, got_pre, *weights)
    got_factors = lax.ppermute(after(other_factors, answered), "section", [(0, 1)])
    send_zero, gather_one, gather_zero = routes_call(1, picks, after_all(masks, answered))
    returned = exchange(answered)
    lower, packed = small_call(
        relay_kernel,
        [KEPT, shape(ROWS, WIDE)],
        [NEAR] * 4,
        [],
        (),
        "relay",
        500_000_000,
        [NEAR] * 2,
        limit=SMALL,
    )(returned, in_vmem(gather_one), in_vmem(send_zero), in_vmem(grads))
    arrived = exchange(packed)
    answered = expert_call(0, arrived, own_factors, got_factors, *weights)
    returned = exchange(answered)
    final = small_call(
        last_kernel,
        shape(TOKENS, MODEL),
        [NEAR] * 3,
        [],
        (),
        "gather_last",
        200_000_000,
        limit=SMALL,
    )(returned, in_vmem(gather_zero), in_vmem(lower))
    other = swapped(jnp.where(section == 0, lower, final))
    first = jnp.where(section == 0, final, other)
    second = jnp.where(section == 0, other, lower)
    return jnp.stack([first, second])[None]


def solution(mesh):
    placed = (
        P(None, "ep", None),
        P("section", None, "ep", None),
        P("section", None, "ep", None),
        P("section", None, "ep", None, None),
        P("section", "ep", None, None),
        P("section", "ep", None, None),
    )
    return jax.shard_map(
        body, mesh=mesh, in_specs=placed, out_specs=P("section", None, "ep", None), check_vma=False
    )
```

```python
import jax
import jax.numpy as jnp
from jax import lax
from jax.experimental import pallas as pl
from jax.experimental.pallas import tpu as pltpu
from jax.sharding import PartitionSpec as P

alpha_glu = 1.702
BF = jnp.bfloat16
F32 = jnp.float32

MODEL = 1536
HIDDEN = 1536
TOKENS = 64
EXPERTS = 64
TOP = 4
CAP = 6
SLOTS = EXPERTS * CAP
PACK = 8
PART = MODEL // 4
WIDE = 3 * PART
ROWS = EXPERTS * PACK
BLOCKS = 16
GROUP_SLOTS = BLOCKS * CAP
GROUP_ROWS = BLOCKS * PACK
GROUPS = EXPERTS // BLOCKS
TILE = 256
STEPS = HIDDEN // TILE
FIRST_WAITS = 2
SECOND_WAITS = 2
PIECES = 4
BIG = 48 * 1024 * 1024
EXPERT_BIG = 48 * 1024 * 1024
FACTORS_BIG = 58 * 1024 * 1024
SMALL = 16 * 1024 * 1024


def iota(shape, axis):
    return lax.broadcasted_iota(jnp.int32, shape, axis)


def dot(a, b, contract=((1,), (0,))):
    return lax.dot_general(a, b, (contract, ((), ())), preferred_element_type=F32)


def fetch(own, got, layer, pairs, sem):
    section = lax.axis_index("section")
    held = [to for to, _ in pairs]
    slots = [slot for _, slot in pairs]

    @pl.when(section == layer)
    def _():
        for source, to, slot in zip(own, held, slots):
            pltpu.make_async_copy(source.at[layer], to, sem.at[slot]).start()

    @pl.when(section != layer)
    def _():
        for source, to, slot in zip(got, held, slots):
            pltpu.make_async_copy(source.at[1 - layer], to, sem.at[slot]).start()


def settle(source, to, sem):
    pltpu.make_async_copy(source, to, sem).wait()


def lanes(value, times):
    return jnp.concatenate([value] * times, axis=1)


def named(ids, shape):
    expert = (iota(shape, 0) // PACK).astype(F32)
    return [ids[k : k + 1, :] == expert for k in range(TOP)]


def slot_counts(picked, lanes):
    earlier = (iota((TOKENS, lanes), 0) < (iota((TOKENS, lanes), 1) % TOKENS)).astype(BF)
    return dot(picked.astype(BF), earlier)


def wanted_slots(shape, part):
    row = iota(shape, 0) % PACK
    main = row
    extra = jnp.where(row >= CAP, 3 * (row - CAP) + part, -1)
    return main, extra


def send_masks(ids, weights):
    shape = (ROWS, 4 * TOKENS)
    hits = named(ids, shape)
    weight = jnp.zeros(shape, F32)
    for k in range(TOP):
        weight = weight + jnp.where(hits[k], weights[k : k + 1, :], 0.0)
    picked = hits[0] | hits[1] | hits[2] | hits[3]
    counts = slot_counts(jnp.where(picked, 1.0, 0.0)[:, :TOKENS], 4 * TOKENS)
    counts = jnp.where(picked, counts, -2.0)
    lead = weight.astype(BF).astype(F32)
    group = iota(shape, 1) // TOKENS
    value = jnp.where(group < 2, lead, weight - lead)
    masks = []
    for part in range(3):
        main, extra = wanted_slots(shape, part)
        slot = jnp.where(group % 2 == 0, main, extra).astype(F32)
        masks.append(jnp.where(counts == slot, value, 0.0).astype(BF))
    return masks


def gather_masks(ids):
    shape = (ROWS, 2 * TOKENS)
    hits = named(ids, shape)
    picked = hits[0] | hits[1] | hits[2] | hits[3]
    counts = slot_counts(jnp.where(picked, 1.0, 0.0)[:, :TOKENS], 2 * TOKENS)
    counts = jnp.where(picked, counts, -2.0)
    group = iota(shape, 1) // TOKENS
    masks = []
    for part in range(3):
        main, extra = wanted_slots(shape, part)
        slot = jnp.where(group == 0, main, extra).astype(F32)
        masks.append(jnp.where(counts == slot, 1.0, 0.0))
    return masks


def send_rows(masks, grads, out_ref):
    last = grads[:, WIDE:]
    for part in range(3):
        here = grads[:, part * PART : (part + 1) * PART]
        rows = jnp.concatenate([here, last, here, last], axis=0)
        out_ref[:, part * PART : (part + 1) * PART] = dot(masks[part], rows).astype(BF)


def gather_rows(masks_ref, packed_ref, grads):
    pieces = []
    last = jnp.zeros((TOKENS, PART), F32)
    for part in range(3):
        both = dot(masks_ref[part], packed_ref[:, part * PART : (part + 1) * PART])
        pieces.append(both[:TOKENS])
        last = last + both[TOKENS:]
    total = jnp.concatenate(pieces + [last], axis=1)
    return (grads.astype(F32) + total).astype(BF)


def first_kernel(own_ids, own_w, got_ids, got_w, grads_ref, out_ref, grads, ids, weights, sem):
    section = lax.axis_index("section")
    fetch((own_ids, own_w), (got_ids, got_w), 1, ((ids, 0), (weights, 1)), sem)
    rows = pltpu.make_async_copy(grads_ref.at[section], grads, sem.at[2])
    rows.start()
    settle(own_ids.at[0], ids, sem.at[0])
    settle(own_w.at[0], weights, sem.at[1])
    masks = send_masks(lanes(ids[...].astype(F32), 4), lanes(weights[...], 4))
    rows.wait()
    send_rows(masks, grads[...], out_ref)


def other_kernel(pre_ref, out_ref, sems):
    section = lax.axis_index("section")
    copies = []
    for piece in range(PIECES):
        here = pl.ds(piece * (SLOTS // PIECES), SLOTS // PIECES)
        copies.append(
            pltpu.make_async_copy(pre_ref.at[1 - section, here], out_ref.at[here], sems.at[piece])
        )
    for copy in copies:
        copy.start()
    for copy in copies:
        copy.wait()


def factors(gate, linear):
    sigmoid = jax.nn.sigmoid(alpha_glu * gate)
    for_gate = (linear + 1.0) * sigmoid * (1.0 + alpha_glu * gate * (1.0 - sigmoid))
    return for_gate, gate * sigmoid


def factors_kernel(pre_ref, first_ref, second_ref, held, made, sems):
    working = lax.axis_index("section") == 0
    size = SLOTS // PIECES
    pieces = [(micro, piece) for micro in (0, 1) for piece in range(PIECES)]

    def into(micro, piece):
        here = pl.ds(piece * size, size)
        return pltpu.make_async_copy(
            pre_ref.at[micro, here], held.at[micro, here], sems.at[0, micro, piece]
        )

    def out(micro, piece):
        here = pl.ds(piece * size, size)
        target = (first_ref, second_ref)[micro]
        return pltpu.make_async_copy(made.at[micro, here], target.at[here], sems.at[1, micro, piece])

    @pl.when(working)
    def _():
        for micro, piece in pieces:
            into(micro, piece).start()

    @pl.when(working)
    def _():
        for micro, piece in pieces:
            into(micro, piece).wait()
            here = slice(piece * size, (piece + 1) * size)
            for_gate, for_up = factors(
                held[micro, here, :HIDDEN].astype(F32), held[micro, here, HIDDEN:].astype(F32)
            )
            made[micro, here, :HIDDEN] = for_gate.astype(BF)
            made[micro, here, HIDDEN:] = for_up.astype(BF)
            out(micro, piece).start()
        for micro, piece in pieces:
            out(micro, piece).wait()


def routes_kernel(mine, own_ids, own_w, got_ids, got_w, *refs):
    send, gather_one, zero_out, ids_one, ids_zero, weights, gather_zero, sem = refs[-8:]
    one = got_ids if mine == 0 else own_ids
    ids, w = (own_ids, own_w) if mine == 0 else (got_ids, got_w)

    @pl.when(lax.axis_index("section") == mine)
    def _():
        picks = [
            pltpu.make_async_copy(one.at[mine], ids_one, sem.at[0]),
            pltpu.make_async_copy(ids.at[mine], ids_zero, sem.at[1]),
            pltpu.make_async_copy(w.at[mine], weights, sem.at[2]),
        ]
        for copy in picks:
            copy.start()
        for copy in picks:
            copy.wait()
        away = pltpu.make_async_copy(gather_zero, zero_out, sem.at[3])
        for part, mask in enumerate(gather_masks(lanes(ids_zero[...].astype(F32), 2))):
            gather_zero[part] = mask.T.astype(BF)
        away.start()
        for part, mask in enumerate(gather_masks(lanes(ids_one[...].astype(F32), 2))):
            gather_one[part] = mask.T.astype(BF)
        masks = send_masks(lanes(ids_zero[...].astype(F32), 4), lanes(weights[...], 4))
        for part, mask in enumerate(masks):
            send[part] = mask
        away.wait()


def relay_kernel(packed_ref, gather, send, grads, lower_ref, out_ref):
    lower = gather_rows(gather, packed_ref, grads[...])
    lower_ref[...] = lower
    send_rows([send[part] for part in range(3)], lower, out_ref)


def last_kernel(packed_ref, gather, grads_ref, out_ref):
    out_ref[...] = gather_rows(gather, packed_ref, grads_ref[...])


def group_masks():
    shape = (GROUP_ROWS, GROUP_SLOTS)
    row, column = iota(shape, 0), iota(shape, 1)
    block = (column * 43) >> 8
    slot = column - CAP * block
    same = (row >> 3) == block
    inner = row & 7
    main = same & (inner == slot)
    extra = [same & (inner >= CAP) & (slot == 3 * (inner - CAP) + part) for part in range(3)]
    return [jnp.where(mask, 1.0, 0.0) for mask in [main] + extra]


def expert_kernel(
    layer, packed_ref, own_pre, got_pre, own_down, got_down, own_up, got_up,
    out_ref, pre, down, up, rows, joined, answers, sems,
):
    section = lax.axis_index("section")

    def copies(step, from_pre, from_down, from_up):
        if step >= STEPS:
            here = pl.ds((step - STEPS) * TILE, TILE)
            return [pltpu.make_async_copy(from_up.at[here], up.at[here], sems.at[0, step])]
        here = pl.ds(step * TILE, TILE)
        there = pl.ds(HIDDEN + step * TILE, TILE)
        return [
            pltpu.make_async_copy(from_down.at[here], down.at[here], sems.at[0, step]),
            pltpu.make_async_copy(from_pre.at[:, here], pre.at[:, here], sems.at[1, step]),
            pltpu.make_async_copy(from_pre.at[:, there], pre.at[:, there], sems.at[2, step]),
        ]

    @pl.when(section == layer)
    def _():
        for step in range(2 * STEPS):
            for copy in copies(step, own_pre.at[1] if layer else own_pre, own_down, own_up):
                copy.start()

    @pl.when(section != layer)
    def _():
        for step in range(2 * STEPS):
            for copy in copies(step, got_pre, got_down, got_up):
                copy.start()

    def finish(step):
        for copy in copies(step, got_pre, got_down, got_up):
            copy.wait()

    masks = group_masks()
    pack_masks = [
        jnp.concatenate([masks[0], masks[1 + part]], axis=1).astype(BF) for part in range(3)
    ]
    open_main = masks[0].T.astype(BF)
    open_last = jnp.concatenate([masks[1 + part].T for part in range(3)], axis=1).astype(BF)
    for group in range(GROUPS):
        taken = packed_ref[group * GROUP_ROWS : (group + 1) * GROUP_ROWS, :]
        target = slice(group * GROUP_SLOTS, (group + 1) * GROUP_SLOTS)
        rows[target, :WIDE] = dot(open_main, taken).astype(BF)
        stacked = jnp.concatenate(
            [taken[:, part * PART : (part + 1) * PART] for part in range(3)], axis=0
        )
        rows[target, WIDE:] = dot(open_last, stacked).astype(BF)

    for step in range(0, STEPS, FIRST_WAITS):
        here = slice(step * TILE, (step + FIRST_WAITS) * TILE)
        there = slice(HIDDEN + step * TILE, HIDDEN + (step + FIRST_WAITS) * TILE)
        for ready in range(step, step + FIRST_WAITS):
            finish(ready)
        back = dot(rows[...], down[here, :], ((1,), (1,)))
        for_gate, for_up = pre[:, here].astype(F32), pre[:, there].astype(F32)
        if layer == 1:
            for_gate, for_up = factors(for_gate, for_up)
        joined[:, here] = (back * for_gate).astype(BF)
        joined[:, there] = (back * for_up).astype(BF)
    for step in range(0, STEPS, SECOND_WAITS):
        here = slice(step * TILE, (step + SECOND_WAITS) * TILE)
        for ready in range(step, step + SECOND_WAITS):
            finish(STEPS + ready)
        answers[:, here] = dot(joined[...], up[here, :], ((1,), (1,))).astype(BF)
    for group in range(GROUPS):
        source = slice(group * GROUP_SLOTS, (group + 1) * GROUP_SLOTS)
        target = slice(group * GROUP_ROWS, (group + 1) * GROUP_ROWS)
        last = answers[source, WIDE:]
        for part in range(3):
            columns = slice(part * PART, (part + 1) * PART)
            both = jnp.concatenate([answers[source, columns], last], axis=0)
            out_ref[target, columns] = dot(pack_masks[part], both).astype(BF)


def shape(*dims, dtype=BF):
    return jax.ShapeDtypeStruct(dims, dtype)


NEAR = pl.BlockSpec(memory_space=pltpu.VMEM)
FAR = pl.BlockSpec(memory_space=pl.ANY)
PICK_IDS = pltpu.VMEM((TOP, TOKENS), jnp.int32)
PICK_WEIGHTS = pltpu.VMEM((TOP, TOKENS), F32)
KEPT = pltpu.VMEM((TOKENS, MODEL), BF)
MASKS = [(3, ROWS, 4 * TOKENS), (3, 2 * TOKENS, ROWS), (3, 2 * TOKENS, ROWS)]


def pinned(value, space):
    return pltpu.with_memory_space_constraint(value, space)


def in_hbm(value):
    return pinned(value, pltpu.MemorySpace.HBM)


def in_vmem(value):
    return pinned(value, pltpu.MemorySpace.VMEM)


def small_call(
    kernel, outs, ins, scratch, copies, name, flops, out_specs=NEAR, limit=BIG, aliases={}, cost=4_000_000
):
    sems = [pltpu.SemaphoreType.DMA(copies)] if copies else []
    return pl.pallas_call(
        kernel,
        out_shape=outs,
        in_specs=ins,
        out_specs=out_specs,
        name=name,
        input_output_aliases=aliases,
        scratch_shapes=scratch + sems,
        compiler_params=pltpu.CompilerParams(vmem_limit_bytes=limit),
        cost_estimate=pl.CostEstimate(flops=flops, bytes_accessed=cost, transcendentals=0),
    )


def factors_call(pre):
    return small_call(
        factors_kernel,
        [pltpu.HBM((SLOTS, 2 * HIDDEN), BF)] * 2,
        [FAR],
        [pltpu.VMEM((2, SLOTS, 2 * HIDDEN), BF)] * 2,
        (2, 2, PIECES),
        "lower_factors",
        20_000_000,
        [FAR] * 2,
        limit=FACTORS_BIG,
    )(in_hbm(pre))


def routes_call(mine, picks, masks):
    held = [in_vmem(mask) for mask in masks[:2]] + [in_hbm(mask) for mask in masks[2:]]
    return small_call(
        lambda *refs: routes_kernel(mine, *refs),
        [pltpu.VMEM(MASKS[0], BF), pltpu.VMEM(MASKS[1], BF), pltpu.HBM(MASKS[2], BF)],
        [FAR] * 4 + [NEAR, NEAR, FAR][: len(masks)],
        [PICK_IDS, PICK_IDS, PICK_WEIGHTS, pltpu.VMEM(MASKS[2], BF)],
        (4,),
        f"routes_section_{mine}",
        1_000_000_000,
        [NEAR, NEAR, FAR],
        limit=SMALL,
        aliases={4 + place: place for place in range(len(masks))},
    )(*picks, *held)


def expert_call(layer, *operands):
    return pl.pallas_call(
        lambda *refs: expert_kernel(layer, *refs),
        out_shape=shape(ROWS, WIDE),
        in_specs=[NEAR] + [FAR] * 6,
        out_specs=NEAR,
        name=f"expert_layer_{layer}",
        scratch_shapes=[
            pltpu.VMEM((SLOTS, 2 * HIDDEN), BF),
            pltpu.VMEM((HIDDEN, MODEL), BF),
            pltpu.VMEM((MODEL, 2 * HIDDEN), BF),
            pltpu.VMEM((SLOTS, MODEL), BF),
            pltpu.VMEM((SLOTS, 2 * HIDDEN), BF),
            pltpu.VMEM((SLOTS, MODEL), BF),
            pltpu.SemaphoreType.DMA((3, 2 * STEPS)),
        ],
        compiler_params=pltpu.CompilerParams(vmem_limit_bytes=EXPERT_BIG),
        cost_estimate=pl.CostEstimate(
            flops=6 * SLOTS * MODEL * HIDDEN, bytes_accessed=20_000_000, transcendentals=0
        ),
    )(*operands)


def exchange(packed):
    return lax.all_to_all(
        packed.reshape(EXPERTS, PACK, WIDE), "ep", split_axis=0, concat_axis=0, tiled=True
    ).reshape(ROWS, WIDE)


def swapped(value):
    return lax.ppermute(value, "section", [(0, 1), (1, 0)])


def after(value, *others):
    return lax.optimization_barrier((value,) + others)[0]


def after_all(values, *others):
    return lax.optimization_barrier(tuple(values) + others)[: len(values)]


def body(top_grads, expert_ids, route_weights, preacts, w_gate_up, w_down):
    section = lax.axis_index("section")
    own_ids = expert_ids[0].transpose(0, 2, 1)
    own_w = route_weights[0].transpose(0, 2, 1)
    own_pre = preacts[0, :, 0]
    own_down, own_up = w_down[0, 0], w_gate_up[0, 0]
    got_ids, got_w = swapped(own_ids), swapped(own_w)
    other_pre = small_call(
        other_kernel, shape(SLOTS, 2 * HIDDEN), [FAR], [], (PIECES,), "other_pre", 1_000_000
    )(own_pre)
    got_down = swapped(after(own_down, got_ids, got_w))
    got_up = swapped(after(own_up, got_ids, got_w))
    got_pre = swapped(other_pre)
    picks = (own_ids, own_w, got_ids, got_w)

    own_factors, other_factors = factors_call(after(own_pre, got_ids, got_w, other_pre))
    masks = routes_call(0, (own_ids, own_w, after(got_ids, own_factors), got_w), ())

    packed, grads = small_call(
        first_kernel,
        [shape(ROWS, WIDE), KEPT],
        [FAR] * 5,
        [PICK_IDS, PICK_WEIGHTS],
        (3,),
        "send_first",
        300_000_000,
        [NEAR] * 2,
        limit=SMALL,
    )(own_ids, own_w, after(got_ids, *masks), got_w, in_hbm(top_grads))
    weights = (own_down, got_down, own_up, got_up)
    arrived = exchange(packed)
    answered = expert_call(1, arrived, own_pre, got_pre, *weights)
    got_factors = lax.ppermute(after(other_factors, answered), "section", [(0, 1)])
    send_zero, gather_one, gather_zero = routes_call(1, picks, after_all(masks, answered))
    returned = exchange(answered)
    lower, packed = small_call(
        relay_kernel,
        [KEPT, shape(ROWS, WIDE)],
        [NEAR] * 4,
        [],
        (),
        "relay",
        500_000_000,
        [NEAR] * 2,
        limit=SMALL,
    )(returned, in_vmem(gather_one), in_vmem(send_zero), in_vmem(grads))
    arrived = exchange(packed)
    answered = expert_call(0, arrived, own_factors, got_factors, *weights)
    returned = exchange(answered)
    final = small_call(
        last_kernel,
        shape(TOKENS, MODEL),
        [NEAR] * 3,
        [],
        (),
        "gather_last",
        200_000_000,
        limit=SMALL,
    )(returned, in_vmem(gather_zero), in_vmem(lower))
    other = swapped(jnp.where(section == 0, lower, final))
    first = jnp.where(section == 0, final, other)
    second = jnp.where(section == 0, other, lower)
    return jnp.stack([first, second])[None]


def solution(mesh):
    placed = (
        P(None, "ep", None),
        P("section", None, "ep", None),
        P("section", None, "ep", None),
        P("section", None, "ep", None, None),
        P("section", "ep", None, None),
        P("section", "ep", None, None),
    )
    return jax.shard_map(
        body, mesh=mesh, in_specs=placed, out_specs=P("section", None, "ep", None), check_vma=False
    )
```
